128 devices in a mesh: slab: 8 (over y, z_lo), plane: 16 (over x, z_hi, core).
Axes of the slice: x: 4, y: 4, z: 4 (z_hi: 2, z_lo: 2; z = z_hi * 2 + z_lo), core: 2. Of those that a mesh axis runs over, the one named last changes fastest.
Arguments:
- right_sides: float32 [8, 256, 32768], P('slab', 'plane'), may hold values from -6 to 6
- diag_tiles: bfloat16 [8, 2, 32768, 2048], P('slab', None, 'plane'), may hold values from -0.09375 to 0.09375
- left_factors: bfloat16 [8, 2, 96, 32768], P('slab', None, None, 'plane'), may hold values from -0.4375 to 0.4375
- source_factors: bfloat16 [8, 2, 96, 32768], P('slab', None, None, 'plane'), may hold values from -0.0234375 to 0.0234375
- trace_factors: bfloat16 [8, 2, 96, 32768], P('slab', None, None, 'plane'), may hold values from -0.01953125 to 0.01953125
Outputs:
- solved: float32 [8, 256, 32768], P('slab', 'plane')
The draws below stay inside these ranges and needn't reach their ends.
All inputs are finite; a program needn't handle non-finite values.
Results may differ from the reference program's by a relative error of at most 0.0029.
Values may be sent and summed in bfloat16 or wider, within the bound.
A program may use at most 128 MiB of HBM per device.

```python
import jax
import jax.numpy as jnp
from jax import lax

TILE = 2048
RANK = 96
NRHS = 128
PLANE_ROWS = 32768
N_SLAB = 8
N_PLANE = 16


def steps_of(key, dims, cuts, least, largest):
    def one(axis_at, parts):
        draws = jax.random.uniform(jax.random.fold_in(jax.random.fold_in(key, 6), axis_at), (parts,), jnp.float32, least / len(cuts), largest / len(cuts))
        return jnp.repeat(jnp.exp(draws), dims[axis_at] // parts).reshape((-1,) + (1,) * (len(dims) - axis_at - 1))

    gain = one(*cuts[0])
    for cut in cuts[1:]:
        gain = gain * one(*cut)
    return gain


def scatter_about(rng, extent, deviation, limit, split=(), kind=jnp.bfloat16):
    level = steps_of(rng, extent, split, -0.22, 0.18) if split else 1.0
    values = jax.random.normal(rng, extent, jnp.float32) * deviation * level
    return jnp.minimum(jnp.maximum(values, -limit), limit).astype(kind)


def setup_inputs(seed: int = 0) -> dict:
    key_list = jax.random.split(jax.random.key(seed), 6)
    right_sides = scatter_about(key_list[0], (N_SLAB, 2 * NRHS, PLANE_ROWS), 1.0, 6.0, ((0, 8), (1, 16)), jnp.float32)
    diag_tiles = scatter_about(key_list[1], (N_SLAB, 2, PLANE_ROWS, TILE), (2 * TILE) ** -0.5, 0.09375, ((0, 8), (2, 16)))
    left_factors = scatter_about(key_list[2], (N_SLAB, 2, RANK, PLANE_ROWS), (2 * RANK) ** -0.5, 0.4375, ((0, 8), (3, 16)))
    source_factors = scatter_about(key_list[3], (N_SLAB, 2, RANK, PLANE_ROWS), (2 * PLANE_ROWS) ** -0.5, 0.0234375, ((0, 8), (3, 16)))
    trace_factors = scatter_about(key_list[4], (N_SLAB, 2, RANK, PLANE_ROWS), (3 * PLANE_ROWS) ** -0.5, 0.01953125, ((0, 8), (3, 16)))
    return {"right_sides": right_sides, "diag_tiles": diag_tiles, "left_factors": left_factors, "source_factors": source_factors, "trace_factors": trace_factors}


def combine_parts(real_part, imag_part):
    half_count = real_part.shape[0] // 2
    upper_rows = real_part[:half_count] - imag_part[half_count:]
    lower_rows = real_part[half_count:] + imag_part[:half_count]
    return jnp.concatenate([upper_rows, lower_rows], axis=0)


def complex_apply(vectors, mat_real, mat_imag, contract_axis, precision):
    contract = (((1,), (contract_axis,)), ((), ()))
    real_part = lax.dot_general(vectors, mat_real, contract, precision=precision, preferred_element_type=jnp.float32)
    imag_part = lax.dot_general(vectors, mat_imag, contract, precision=precision, preferred_element_type=jnp.float32)
    return combine_parts(real_part, imag_part)


def reference(right_sides, diag_tiles, left_factors, source_factors, trace_factors):
    precise = lax.Precision.HIGHEST
    outputs = []
    previous = jnp.zeros((right_sides.shape[1], right_sides.shape[2]), jnp.float32)
    for slab_index in range(N_SLAB):
        half_sides = right_sides[slab_index].astype(jnp.bfloat16)
        tiled_rows = half_sides.reshape(2 * NRHS, N_PLANE, TILE).astype(jnp.float32)
        tile_block = diag_tiles[slab_index].reshape(2, N_PLANE, TILE, TILE).astype(jnp.float32)
        real_part = jnp.einsum("cpk,pjk->cpj", tiled_rows, tile_block[0], precision=precise)
        imag_part = jnp.einsum("cpk,pjk->cpj", tiled_rows, tile_block[1], precision=precise)
        local_part = combine_parts(real_part, imag_part).reshape(2 * NRHS, PLANE_ROWS)
        source_term = complex_apply(half_sides, source_factors[slab_index, 0], source_factors[slab_index, 1], 1, None)
        trace_real = trace_factors[slab_index, 0].astype(jnp.float32)
        trace_imag = trace_factors[slab_index, 1].astype(jnp.float32)
        mixing = source_term + complex_apply(previous, trace_real, trace_imag, 1, precise)
        left_real = left_factors[slab_index, 0].astype(jnp.float32)
        left_imag = left_factors[slab_index, 1].astype(jnp.float32)
        solved = local_part + complex_apply(mixing, left_real, left_imag, 0, precise)
        outputs.append(solved)
        previous = solved
    return jnp.stack(outputs)
```

```python
import functools

import jax
import jax.numpy as jnp
from jax import lax
from jax.experimental import pallas as pl
from jax.experimental.pallas import tpu as pltpu
from jax.sharding import PartitionSpec as P

MESH = pl.DeviceIdType.MESH
F32 = jnp.float32
BF16 = jnp.bfloat16
PAD = 128
CHUNKS = 8
X, T, RM, AM, A1, A2, RS, RP, V1, V2, V4, AV, E = range(13)
N_GROUPS = 13


def split(value):
    high = value.astype(BF16)
    low = (value - high.astype(F32)).astype(BF16)
    return high, low


def nt_dot(rows, mat):
    return lax.dot_general(rows, mat, (((1,), (1,)), ((), ())), preferred_element_type=F32)


def nn_dot(rows, mat):
    return lax.dot_general(rows, mat, (((1,), (0,)), ((), ())), preferred_element_type=F32)


def from_products(both, half):
    real = both[:half, :PAD] - both[half:, PAD:]
    imag = both[half:, :PAD] + both[:half, PAD:]
    return jnp.concatenate([real, imag], axis=1)


def expanded(top):
    real, imag = top[:, :PAD], top[:, PAD:]
    return jnp.concatenate([top, jnp.concatenate([-imag, real], axis=1)], axis=0)


def split_dot(rows, high, low):
    count = rows.shape[0]
    rows_high = rows.astype(BF16).astype(F32)
    stacked = jnp.concatenate([rows_high, rows - rows_high], axis=0).astype(BF16)
    first = nn_dot(stacked, high)
    second = nn_dot(stacked, low)
    return first[:count] + first[count:] + second[:count] + second[count:]


def kernel(
    n_slab, n_plane, rank,
    rs_ref, d_ref, l_ref, sf_ref, t_ref, o_ref,
    d_vm, rs_vm, x_send, x_recv, t_vm, l_vm, s_vm, local, e_send,
    m_part, m_recv, a1, a1_prev, a2, a2_prev, a_high, a_low,
    s_part, s_recv, p_part, p_recv, v_send, v_recv, mix,
    d_sem, rs_sem, in_sem, own_sem, send_sem, recv_sem,
):
    s = lax.axis_index("slab")
    p = lax.axis_index("plane")
    tile = d_ref.shape[2]
    step = tile // CHUNKS
    half = 8 * n_plane

    def remote(src, dst, group, device):
        return pltpu.make_async_remote_copy(
            src_ref=src, dst_ref=dst, send_sem=send_sem.at[group], recv_sem=recv_sem.at[group],
            device_id=device, device_id_type=MESH,
        )

    def await_recv(ref, group):
        remote(ref, ref, group, (s, lax.rem(p + 1, n_plane))).wait_recv()

    def await_send(ref, group):
        remote(ref, ref, group, (s, lax.rem(p + 1, n_plane))).wait_send()

    def to_plane(src_of, dst, group):
        def one(i, carry):
            q = lax.rem(p + i, n_plane)
            remote(src_of(q), dst, group, (s, q)).start()
            return carry
        lax.fori_loop(1, n_plane, one, 0)

    def to_next_slab(src, dst, group):
        def one(i, carry):
            q = lax.rem(p + i, n_plane)
            remote(src.at[q], dst, group, (s + 1, q)).start()
            return carry
        lax.fori_loop(0, n_plane, one, 0)

    def rs_copy(q):
        return pltpu.make_async_copy(
            rs_ref.at[0, :, pl.ds(pl.multiple_of(q * tile, tile), tile)], rs_vm.at[q], rs_sem.at[q]
        )

    def start_rs(i, carry):
        rs_copy(lax.rem(p + i, n_plane)).start()
        return carry
    lax.fori_loop(1, n_plane + 1, start_rs, 0)
    l_copy = pltpu.make_async_copy(l_ref.at[0], l_vm.at[:, pl.ds(0, rank), :], in_sem.at[0])
    s_copy = pltpu.make_async_copy(sf_ref.at[0], s_vm.at[:, pl.ds(0, rank), :], in_sem.at[1])
    l_copy.start()
    s_copy.start()

    def d_copy(j):
        rows = pl.ds(pl.multiple_of(j * step, step), step)
        return pltpu.make_async_copy(d_ref.at[0, :, rows, :], d_vm.at[:, rows, :], d_sem.at[j])

    def start_d(j, carry):
        d_copy(j).start()
        return carry
    lax.fori_loop(0, CHUNKS, start_d, 0)
    for padded in (t_vm, l_vm, s_vm):
        padded[:, rank:, :] = jnp.zeros((2, PAD - rank, tile), BF16)

    barrier = pltpu.get_barrier_semaphore()

    def greet(device):
        pl.semaphore_signal(barrier, inc=1, device_id=device, device_id_type=MESH)

    def greet_plane(i, carry):
        greet((s, lax.rem(p + i, n_plane)))
        return carry
    lax.fori_loop(1, n_plane, greet_plane, 0)
    pl.when(s < n_slab - 1)(lambda: greet((s + 1, p)))
    for distance in (1, 2, 4):
        pl.when(s >= distance)(functools.partial(lambda d: greet((s - d, p)), distance))
    expected = n_plane - 1 + (s >= 1).astype(jnp.int32)
    for distance in (1, 2, 4):
        expected = expected + (s + distance < n_slab).astype(jnp.int32)
    pl.semaphore_wait(barrier, expected)

    t_copy = remote(t_ref.at[0], t_vm.at[:, pl.ds(0, rank), :], T, (s - 1, p))
    pl.when(s >= 1)(t_copy.start)

    def cast_block(q):
        rs_copy(q).wait()
        return rs_vm[q].astype(BF16)

    zbit = lax.rem(p // 2, 2)

    def send_same(i, carry):
        q = lax.rem(p + i, n_plane)
        x_send[q] = cast_block(q)

        @pl.when(lax.rem(q // 2, 2) == zbit)
        def _():
            remote(x_send.at[q], x_recv.at[p], X, (s, q)).start()
        return carry
    lax.fori_loop(1, n_plane, send_same, 0)
    x_recv[p] = cast_block(p)
    pl.when(s >= 1)(t_copy.wait_send)

    def send_other(i, carry):
        q = lax.rem(p + i, n_plane)

        @pl.when(lax.rem(q // 2, 2) != zbit)
        def _():
            remote(x_send.at[q], x_recv.at[p], X, (s, q)).start()
        return carry
    lax.fori_loop(1, n_plane, send_other, 0)

    l_copy.wait()

    @pl.when(s < n_slab - 1)
    def _():
        t_copy.wait_recv()
        products = nt_dot(l_vm[...].reshape(2 * PAD, tile), t_vm[...].reshape(2 * PAD, tile))
        m_part[...] = from_products(products, PAD).reshape(m_part.shape)
        to_next_slab(m_part, m_recv.at[p], RM)

    def keep(index, top):
        square = expanded(top)
        high, low = split(square)
        a_high[index] = high
        a_low[index] = low

    others = pl.ds(0, n_plane - 1)

    @pl.when(s >= 1)
    def _():
        await_recv(m_recv, RM)
        a1[p] = jnp.sum(m_recv[...], axis=0)
        to_plane(lambda q: a1.at[p], a1.at[p], AM)
        await_recv(a1.at[others], AM)
        keep(0, a1[...].reshape(PAD, 2 * PAD))

    a1_copy = remote(a1, a1_prev, A1, (s + 1, p))
    pl.when((s >= 1) & (s < n_slab - 1))(a1_copy.start)

    await_recv(x_recv.at[others], X)
    x = x_recv[...].reshape(2 * half, tile)
    s_copy.wait()
    s_part[...] = from_products(nt_dot(x, s_vm[...].reshape(2 * PAD, tile)), half).reshape(s_part.shape)
    s_recv[p] = s_part[p]
    to_plane(lambda q: s_part.at[q], s_recv.at[p], RS)

    def local_chunk(j, carry):
        d_copy(j).wait()
        rows = pl.ds(pl.multiple_of(j * step, step), step)
        real = nt_dot(x_recv[...].reshape(2 * half, tile), d_vm[0, rows, :])
        imag = nt_dot(x_recv[...].reshape(2 * half, tile), d_vm[1, rows, :])
        local[:half, rows] = real[:half] - imag[half:]
        local[half:, rows] = real[half:] + imag[:half]
        return carry
    lax.fori_loop(0, CHUNKS, local_chunk, 0)

    @pl.when(s < n_slab - 1)
    def _():
        high, low = split(local[...])
        t_rows = t_vm[...].reshape(2 * PAD, tile)
        p_part[...] = from_products(nt_dot(high, t_rows) + nt_dot(low, t_rows), half).reshape(p_part.shape)
        to_next_slab(p_part, p_recv.at[p], RP)

    a2_copy = remote(a2, a2_prev, A2, (s + 2, p))

    @pl.when(s >= 2)
    def _():
        await_recv(a1_prev, A1)
        a2[...] = split_dot(a1_prev[...].reshape(PAD, 2 * PAD), a_high[0], a_low[0]).reshape(a2.shape)
        pl.when(s < n_slab - 2)(a2_copy.start)
        keep(1, a2[...].reshape(PAD, 2 * PAD))

    await_recv(s_recv.at[others], RS)
    v_send[0] = jnp.sum(s_recv[...], axis=0)

    @pl.when(s >= 1)
    def _():
        await_recv(p_recv, RP)
        v_send[0] = v_send[0] + jnp.sum(p_recv[...], axis=0)

    v_copies = []
    for index, (distance, group) in enumerate(((1, V1), (2, V2), (4, V4))):
        copy = remote(v_send.at[index], v_recv.at[index], group, (s + distance, p))
        v_copies.append(copy)
        pl.when(s + distance < n_slab)(copy.start)
        if distance == 4:
            @pl.when(s >= 4)
            def _():
                await_recv(a2_prev, A2)
                top = split_dot(a2_prev[...].reshape(PAD, 2 * PAD), a_high[1], a_low[1])
                keep(2, top)
        v_send[index + 1] = v_send[index]

        @pl.when(s >= distance)
        def _():
            copy.wait_recv()
            v_send[index + 1] = v_send[index] + split_dot(v_recv[index], a_high[index], a_low[index])

    mix[p] = v_send[3]
    to_plane(lambda q: mix.at[p], mix.at[p], AV)
    await_recv(mix.at[others], AV)
    mixing = mix[...].reshape(half, 2 * PAD)
    real, imag = mixing[:, :PAD], mixing[:, PAD:]
    square = jnp.concatenate(
        [jnp.concatenate([real, -imag], axis=1), jnp.concatenate([imag, real], axis=1)], axis=0
    )
    high, low = split(square)
    l_rows = l_vm[...].reshape(2 * PAD, tile)
    solved = local[...] + nn_dot(high, l_rows) + nn_dot(low, l_rows)
    e_send[...] = solved.astype(BF16).reshape(e_send.shape)

    mine = pl.ds(pl.multiple_of(p * tile, tile), tile)
    own = pltpu.make_async_copy(e_send.at[p], o_ref.at[:, mine], own_sem)
    own.start()
    to_plane(lambda q: e_send.at[q], o_ref.at[:, mine], E)
    own.wait()

    await_send(x_send.at[others], X)
    await_send(s_part.at[others], RS)
    await_send(mix.at[others], AV)

    @pl.when(s < n_slab - 1)
    def _():
        await_send(m_part, RM)
        await_send(p_part, RP)

    @pl.when(s >= 1)
    def _():
        await_send(a1.at[others], AM)
        pl.when(s < n_slab - 1)(a1_copy.wait_send)
    pl.when((s >= 2) & (s < n_slab - 2))(a2_copy.wait_send)
    for distance, copy in zip((1, 2, 4), v_copies):
        pl.when(s + distance < n_slab)(copy.wait_send)
    await_send(e_send.at[others], E)
    await_recv(o_ref.at[:, pl.ds(0, (n_plane - 1) * tile)], E)


def solution(mesh):
    n_slab, n_plane = mesh.shape["slab"], mesh.shape["plane"]

    def body(right_sides, diag_tiles, left_factors, source_factors, trace_factors):
        tile, rank = diag_tiles.shape[2], left_factors.shape[2]
        columns = right_sides.shape[1]
        small = pltpu.VMEM((n_plane, 8, 2 * PAD), F32)
        ranks = pltpu.VMEM((n_plane, PAD // n_plane, 2 * PAD), F32)
        padded = pltpu.VMEM((2, PAD, tile), BF16)
        blocks = pltpu.VMEM((n_plane, columns, tile), BF16)
        squares = pltpu.VMEM((3, 2 * PAD, 2 * PAD), BF16)
        out = pl.pallas_call(
            functools.partial(kernel, n_slab, n_plane, rank),
            out_shape=jax.ShapeDtypeStruct((columns, n_plane * tile), BF16),
            in_specs=[pl.BlockSpec(memory_space=pl.ANY)] * 5,
            out_specs=pl.BlockSpec(memory_space=pl.ANY),
            scratch_shapes=[
                pltpu.VMEM((2, tile, tile), BF16),
                pltpu.VMEM((n_plane, columns, tile), F32),
                blocks, blocks, padded, padded, padded,
                pltpu.VMEM((columns * n_plane, tile), F32),
                blocks,
                ranks, ranks, ranks, ranks, ranks, ranks, squares, squares,
                small, small, small, small,
                pltpu.VMEM((4, 8, 2 * PAD), F32),
                pltpu.VMEM((3, 8, 2 * PAD), F32),
                small,
                pltpu.SemaphoreType.DMA((CHUNKS,)),
                pltpu.SemaphoreType.DMA((n_plane,)),
                pltpu.SemaphoreType.DMA((2,)),
                pltpu.SemaphoreType.DMA,
                pltpu.SemaphoreType.DMA((N_GROUPS,)),
                pltpu.SemaphoreType.DMA((N_GROUPS,)),
            ],
            compiler_params=pltpu.CompilerParams(
                collective_id=0, has_side_effects=True, vmem_limit_bytes=60 * 2**20
            ),
            name="sweep",
        )(right_sides, diag_tiles, left_factors, source_factors, trace_factors)
        return out.astype(F32)[None]

    placed = (
        P("slab", "plane", None),
        P("slab", None, "plane", None),
        P("slab", None, None, "plane"),
        P("slab", None, None, "plane"),
        P("slab", None, None, "plane"),
    )
    return jax.shard_map(
        body, mesh=mesh, in_specs=placed, out_specs=P("slab", "plane", None), check_vma=False
    )
```

```python
import functools

import jax
import jax.numpy as jnp
from jax import lax
from jax.experimental import pallas as pl
from jax.experimental.pallas import tpu as pltpu
from jax.sharding import PartitionSpec as P

MESH = pl.DeviceIdType.MESH
F32 = jnp.float32
BF16 = jnp.bfloat16
PAD = 128
CHUNKS = 8
X0, X1, T, RM, AM, B1, B2, C2, G2, G4, RS, RP, V1, V2, V3, V4, AV, E = range(18)
N_GROUPS = 18


def split(value):
    high = value.astype(BF16)
    low = (value - high.astype(F32)).astype(BF16)
    return high, low


def nt_dot(rows, mat):
    return lax.dot_general(rows, mat, (((1,), (1,)), ((), ())), preferred_element_type=F32)


def nn_dot(rows, mat):
    return lax.dot_general(rows, mat, (((1,), (0,)), ((), ())), preferred_element_type=F32)


def from_products(both):
    half = both.shape[0] // 2
    real = both[:half, :PAD] - both[half:, PAD:]
    imag = both[half:, :PAD] + both[:half, PAD:]
    return jnp.concatenate([real, imag], axis=1)


def expanded(top):
    real, imag = top[:, :PAD], top[:, PAD:]
    return jnp.concatenate([top, jnp.concatenate([-imag, real], axis=1)], axis=0)


def stacked_halves(rows):
    rows_high = rows.astype(BF16).astype(F32)
    return jnp.concatenate([rows_high, rows - rows_high], axis=0).astype(BF16)


def split_dot(rows, high, low):
    count = rows.shape[0]
    stacked = stacked_halves(rows)
    total = nn_dot(stacked, high) + nn_dot(stacked, low)
    return total[:count] + total[count:]


def kernel(
    n_slab, n_plane, rank,
    rs_ref, d_ref, l_ref, sf_ref, t_ref, o_ref,
    d_vm, rs_vm, x_send, x_recv, t_vm, l_vm, s_vm, local, e_send,
    m_part, m_recv, a1, a2, a4, b1, b2, c2, a_high, a_low,
    s_part, s_recv, p_part, p_recv, v_send, v_recv, mix,
    d_sem, rs_sem, in_sem, own_sem, send_sem, recv_sem,
):
    s = lax.axis_index("slab")
    p = lax.axis_index("plane")
    tile = d_ref.shape[2]
    step = tile // CHUNKS
    side = n_plane // 2
    run = max(1, n_plane // 8)

    def device_at(k):
        slot = lax.rem(k, side)
        return (slot // run) * 2 * run + (k // side) * run + lax.rem(slot, run)

    my_side = lax.rem(p // run, 2)
    my_slot = (p // (2 * run)) * run + lax.rem(p, run)
    far_side = 1 - my_side
    me = my_side * side + my_slot

    def remote(src, dst, group, device):
        return pltpu.make_async_remote_copy(
            src_ref=src, dst_ref=dst, send_sem=send_sem.at[group], recv_sem=recv_sem.at[group],
            device_id=device, device_id_type=MESH,
        )

    peer = (s, lax.rem(p + 1, n_plane))

    def await_recv(ref, group):
        remote(ref, ref, group, peer).wait_recv()

    def await_send(ref, group):
        remote(ref, ref, group, peer).wait_send()

    others = pl.ds(0, n_plane - 1)
    near_others = pl.ds(0, side - 1)
    all_far = pl.ds(0, side)

    def to_plane(src, dst, group):
        def one(i, carry):
            remote(src, dst, group, (s, device_at(lax.rem(me + i, n_plane)))).start()
            return carry
        lax.fori_loop(1, n_plane, one, 0)

    def place(which, i):
        return which * side + lax.rem(my_slot + i, side)

    def blocks_of(which, first, last, src, dst, group, slab):
        def one(i, carry):
            k = place(which, i)
            remote(src.at[k], dst, group, (slab, device_at(k))).start()
            return carry
        lax.fori_loop(first, last, one, 0)

    def rs_copy(k):
        lanes = pl.ds(pl.multiple_of(device_at(k) * tile, tile), tile)
        return pltpu.make_async_copy(rs_ref.at[0, :, lanes], rs_vm.at[k], rs_sem.at[k])

    def start_rs(which):
        def one(i, carry):
            rs_copy(place(which, i)).start()
            return carry
        lax.fori_loop(0, side, one, 0)

    start_rs(my_side)
    s_copy = pltpu.make_async_copy(sf_ref.at[0], s_vm.at[:, pl.ds(0, rank), :], in_sem.at[1])
    s_copy.start()

    def d_copy(j):
        rows = pl.ds(pl.multiple_of(j * step, step), step)
        return pltpu.make_async_copy(d_ref.at[0, :, rows, :], d_vm.at[:, rows, :], d_sem.at[j])

    def start_d(j, carry):
        d_copy(j).start()
        return carry

    v_recv[...] = jnp.zeros_like(v_recv)
    barrier = pltpu.get_barrier_semaphore()

    def greet(device):
        pl.semaphore_signal(barrier, inc=1, device_id=device, device_id_type=MESH)

    def greet_plane(i, carry):
        greet((s, lax.rem(p + i, n_plane)))
        return carry
    lax.fori_loop(1, n_plane, greet_plane, 0)
    pl.when(s < n_slab - 1)(lambda: greet((s + 1, p)))
    for distance in (1, 2, 3, 4):
        pl.when(s >= distance)(functools.partial(lambda d: greet((s - d, p)), distance))

    start_rs(far_side)
    lax.fori_loop(0, CHUNKS, start_d, 0)
    l_copy = pltpu.make_async_copy(l_ref.at[0], l_vm.at[:, pl.ds(0, rank), :], in_sem.at[0])
    l_copy.start()
    for padded in (t_vm, l_vm, s_vm):
        padded[:, rank:, :] = jnp.zeros((2, PAD - rank, tile), BF16)

    a_high[...] = jnp.zeros_like(a_high)
    a_low[...] = jnp.zeros_like(a_low)

    expected = n_plane - 1 + (s >= 1).astype(jnp.int32)
    for distance in (1, 2, 3, 4):
        expected = expected + (s + distance < n_slab).astype(jnp.int32)
    pl.semaphore_wait(barrier, expected)

    t_copy = remote(t_ref.at[0], t_vm.at[:, pl.ds(0, rank), :], T, (s - 1, p))
    pl.when(s >= 1)(t_copy.start)

    def near_block(i, carry):
        k = place(my_side, i)
        rs_copy(k).wait()
        x_send[k] = rs_vm[k].astype(BF16)
        remote(x_send.at[k], x_recv.at[me], X0, (s, device_at(k))).start()
        return carry
    lax.fori_loop(1, side, near_block, 0)
    rs_copy(me).wait()
    x_recv[me] = rs_vm[me].astype(BF16)

    def far_cast(i, carry):
        k = place(far_side, i)
        rs_copy(k).wait()
        x_send[k] = rs_vm[k].astype(BF16)
        return carry
    lax.fori_loop(0, side, far_cast, 0)

    def far_blocks(first, last):
        blocks_of(far_side, first, last, x_send, x_recv.at[me], X1, s)

    def side_rows(which):
        return pl.ds(which * side, side)

    def source_part(which):
        x = x_recv[side_rows(which)].reshape(side * 16, tile)
        products = from_products(nt_dot(x, s_vm[...].reshape(2 * PAD, tile)))
        s_part[side_rows(which)] = products.reshape(side, 8, 2 * PAD)

    def local_part(which, first):
        def chunk(j, carry):
            if first:
                d_copy(j).wait()
            rows = pl.ds(pl.multiple_of(j * step, step), step)
            x = x_recv[side_rows(which)].reshape(side * 16, tile)
            real = nt_dot(x, d_vm[0, rows, :])
            imag = nt_dot(x, d_vm[1, rows, :])
            local[which, :side * 8, rows] = real[:side * 8] - imag[side * 8:]
            local[which, side * 8:, rows] = real[side * 8:] + imag[:side * 8]
            return carry
        lax.fori_loop(0, CHUNKS, chunk, 0)

    def trace_part(which):
        high, low = split(local[which])
        products = nt_dot(jnp.concatenate([high, low], axis=0), t_vm[...].reshape(2 * PAD, tile))
        both = from_products(products[:side * 16] + products[side * 16:])
        p_part[side_rows(which)] = both.reshape(side, 8, 2 * PAD)
        blocks_of(which, 0, side, p_part, p_recv.at[me], RP, s + 1)

    await_recv(x_recv.at[near_others], X0)
    s_copy.wait()
    source_part(my_side)
    s_recv[me] = s_part[me]
    blocks_of(my_side, 1, side, s_part, s_recv.at[me], RS, s)
    local_part(my_side, True)
    l_copy.wait()

    pl.when(s >= 1)(t_copy.wait_send)

    @pl.when(s < n_slab - 1)
    def _():
        t_copy.wait_recv()
        products = nt_dot(l_vm[...].reshape(2 * PAD, tile), t_vm[...].reshape(2 * PAD, tile))
        m_part[...] = from_products(products).reshape(m_part.shape)

        def one(i, carry):
            k = lax.rem(me + i, n_plane)
            remote(m_part.at[k], m_recv.at[me], RM, (s + 1, device_at(k))).start()
            return carry
        lax.fori_loop(0, n_plane, one, 0)

    far_blocks(0, 3 * side // 8)

    def keep(index, top):
        high, low = split(expanded(top.reshape(PAD, 2 * PAD)))
        a_high[index] = high
        a_low[index] = low

    b1_copy = remote(a1.at[me], b1, B1, (s + 1, p))
    b2_copy = remote(a1.at[me], b2, B2, (s + 2, p))
    c2_copy = remote(a2.at[me], c2, C2, (s + 2, p))
    pl.when(s < n_slab - 1)(lambda: trace_part(my_side))

    @pl.when(s >= 1)
    def _():
        await_recv(m_recv, RM)
        a1[me] = jnp.sum(m_recv[...], axis=0)
        to_plane(a1.at[me], a1.at[me], AM)
        pl.when(s + 1 < n_slab)(b1_copy.start)
        pl.when(s + 2 < n_slab)(b2_copy.start)

    far_blocks(3 * side // 8, 6 * side // 8)

    @pl.when(s >= 1)
    def _():
        await_recv(a1.at[others], AM)
        keep(0, a1[...])

    @pl.when(s >= 2)
    def _():
        await_recv(b1, B1)
        a2[me] = split_dot(b1[...], a_high[0], a_low[0])
        to_plane(a2.at[me], a2.at[me], G2)
        pl.when(s + 2 < n_slab)(c2_copy.start)

    far_blocks(6 * side // 8, side)

    @pl.when(s >= 2)
    def _():
        await_recv(a2.at[others], G2)
        keep(1, a2[...])

    @pl.when(s >= 3)
    def _():
        await_recv(b2, B2)
        a4[me, 0] = split_dot(b2[...], a_high[1], a_low[1])
        a4[me, 1] = jnp.zeros(b2.shape, F32)

        @pl.when(s >= 4)
        def _():
            await_recv(c2, C2)
            a4[me, 1] = split_dot(c2[...], a_high[1], a_low[1])
        to_plane(a4.at[me], a4.at[me], G4)

    await_recv(x_recv.at[all_far], X1)
    local_part(far_side, False)
    pl.when(s < n_slab - 1)(lambda: trace_part(far_side))
    source_part(far_side)
    blocks_of(far_side, 0, side, s_part, s_recv.at[me], RS, s)

    @pl.when(s >= 3)
    def _():
        await_recv(a4.at[others], G4)
        keep(2, a4[:, 0])
        keep(3, a4[:, 1])

    await_recv(s_recv.at[others], RS)
    v_send[0] = jnp.sum(s_recv[...], axis=0)

    @pl.when(s >= 1)
    def _():
        await_recv(p_recv, RP)
        v_send[0] = v_send[0] + jnp.sum(p_recv[...], axis=0)

    v_copies = []
    for index, (distance, group) in enumerate(((1, V1), (2, V2), (3, V3), (4, V4))):
        source = v_send.at[0 if distance < 4 else 1]
        v_copies.append(remote(source, v_recv.at[index], group, (s + distance, p)))
    for distance in (1, 2, 3):
        pl.when(s + distance < n_slab)(v_copies[distance - 1].start)
    for distance in (1, 2, 3):
        pl.when(s >= distance)(v_copies[distance - 1].wait_recv)
    total = v_send[0]
    for index in range(3):
        total = total + split_dot(v_recv[index], a_high[index], a_low[index])
    v_send[1] = total
    mix[me] = total
    pl.when(s + 4 < n_slab)(v_copies[3].start)

    @pl.when(s >= 4)
    def _():
        v_copies[3].wait_recv()
        mix[me] = v_send[1] + split_dot(v_recv[3], a_high[3], a_low[3])

    to_plane(mix.at[me], mix.at[me], AV)
    await_recv(mix.at[others], AV)

    mine = pl.ds(pl.multiple_of(p * tile, tile), tile)

    def solve_side(which):
        mixing = mix[side_rows(which)].reshape(side * 8, 2 * PAD)
        real, imag = mixing[:, :PAD], mixing[:, PAD:]
        square = jnp.concatenate(
            [jnp.concatenate([real, -imag], axis=1), jnp.concatenate([imag, real], axis=1)], axis=0
        )
        both = nn_dot(stacked_halves(square), l_vm[...].reshape(2 * PAD, tile))
        solved = local[which] + both[:side * 16] + both[side * 16:]
        e_send[side_rows(which)] = solved.astype(BF16).reshape(side, 16, tile)

    solve_side(far_side)
    blocks_of(far_side, 0, side, e_send, o_ref.at[:, mine], E, s)
    solve_side(my_side)
    blocks_of(my_side, 1, side, e_send, o_ref.at[:, mine], E, s)
    own = pltpu.make_async_copy(e_send.at[me], o_ref.at[:, mine], own_sem)
    own.start()

    await_send(x_send.at[near_others], X0)
    await_send(x_send.at[all_far], X1)
    await_send(s_part.at[others], RS)
    await_send(mix.at[others], AV)

    @pl.when(s < n_slab - 1)
    def _():
        await_send(m_part, RM)
        await_send(p_part, RP)

    @pl.when(s >= 1)
    def _():
        await_send(a1.at[others], AM)
        pl.when(s + 1 < n_slab)(b1_copy.wait_send)
        pl.when(s + 2 < n_slab)(b2_copy.wait_send)

    @pl.when(s >= 2)
    def _():
        await_send(a2.at[others], G2)
        pl.when(s + 2 < n_slab)(c2_copy.wait_send)
    pl.when(s >= 3)(lambda: await_send(a4.at[others], G4))
    for distance in (1, 2, 3, 4):
        pl.when(s + distance < n_slab)(v_copies[distance - 1].wait_send)
    own.wait()
    await_send(e_send.at[others], E)
    await_recv(o_ref.at[:, pl.ds(0, (n_plane - 1) * tile)], E)


def solution(mesh):
    n_slab, n_plane = mesh.shape["slab"], mesh.shape["plane"]

    def body(right_sides, diag_tiles, left_factors, source_factors, trace_factors):
        tile, rank = diag_tiles.shape[2], left_factors.shape[2]
        columns = right_sides.shape[1]
        part = PAD // n_plane
        small = pltpu.VMEM((n_plane, 8, 2 * PAD), F32)
        ranks = pltpu.VMEM((n_plane, part, 2 * PAD), F32)
        one = pltpu.VMEM((part, 2 * PAD), F32)
        padded = pltpu.VMEM((2, PAD, tile), BF16)
        blocks = pltpu.VMEM((n_plane, columns, tile), BF16)
        squares = pltpu.VMEM((4, 2 * PAD, 2 * PAD), BF16)
        out = pl.pallas_call(
            functools.partial(kernel, n_slab, n_plane, rank),
            out_shape=jax.ShapeDtypeStruct((columns, n_plane * tile), BF16),
            in_specs=[pl.BlockSpec(memory_space=pl.ANY)] * 5,
            out_specs=pl.BlockSpec(memory_space=pl.ANY),
            scratch_shapes=[
                pltpu.VMEM((2, tile, tile), BF16),
                pltpu.VMEM((n_plane, columns, tile), F32),
                blocks, blocks, padded, padded, padded,
                pltpu.VMEM((2, columns * n_plane // 2, tile), F32),
                blocks,
                ranks, ranks, ranks, ranks, pltpu.VMEM((n_plane, 2, part, 2 * PAD), F32),
                one, one, one, squares, squares,
                small, small, small, small,
                pltpu.VMEM((2, 8, 2 * PAD), F32),
                pltpu.VMEM((4, 8, 2 * PAD), F32),
                small,
                pltpu.SemaphoreType.DMA((CHUNKS,)),
                pltpu.SemaphoreType.DMA((n_plane,)),
                pltpu.SemaphoreType.DMA((2,)),
                pltpu.SemaphoreType.DMA,
                pltpu.SemaphoreType.DMA((N_GROUPS,)),
                pltpu.SemaphoreType.DMA((N_GROUPS,)),
            ],
            compiler_params=pltpu.CompilerParams(
                collective_id=0, has_side_effects=True, vmem_limit_bytes=60 * 2**20
            ),
            name="sweep",
        )(right_sides, diag_tiles, left_factors, source_factors, trace_factors)
        return out.astype(F32)[None]

    placed = (
        P("slab", "plane", None),
        P("slab", None, "plane", None),
        P("slab", None, None, "plane"),
        P("slab", None, None, "plane"),
        P("slab", None, None, "plane"),
    )
    return jax.shard_map(
        body, mesh=mesh, in_specs=placed, out_specs=P("slab", "plane", None), check_vma=False
    )
```

```python
import functools

import jax
import jax.numpy as jnp
from jax import lax
from jax.experimental import pallas as pl
from jax.experimental.pallas import tpu as pltpu
from jax.sharding import PartitionSpec as P

MESH = pl.DeviceIdType.MESH
F32 = jnp.float32
BF16 = jnp.bfloat16
PAD = 128
CHUNKS = 8
X0, X1, T, RM, AM, B1, B2, C2, G2, G4, RS, V1, V2, V3, V4, VB, AV, E = range(18)
N_GROUPS = 18


def split(value):
    high = value.astype(BF16)
    low = (value - high.astype(F32)).astype(BF16)
    return high, low


def nt_dot(rows, mat):
    return lax.dot_general(rows, mat, (((1,), (1,)), ((), ())), preferred_element_type=F32)


def nn_dot(rows, mat):
    return lax.dot_general(rows, mat, (((1,), (0,)), ((), ())), preferred_element_type=F32)


def from_products(both):
    half = both.shape[0] // 2
    real = both[:half, :PAD] - both[half:, PAD:]
    imag = both[half:, :PAD] + both[:half, PAD:]
    return jnp.concatenate([real, imag], axis=1)


def expanded(top):
    real, imag = top[:, :PAD], top[:, PAD:]
    return jnp.concatenate([top, jnp.concatenate([-imag, real], axis=1)], axis=0)


def stacked_halves(rows):
    rows_high = rows.astype(BF16).astype(F32)
    return jnp.concatenate([rows_high, rows - rows_high], axis=0).astype(BF16)


def split_dot(rows, high, low):
    count = rows.shape[0]
    stacked = stacked_halves(rows)
    total = nn_dot(stacked, high) + nn_dot(stacked, low)
    return total[:count] + total[count:]


def kernel(
    n_slab, n_plane, rank,
    rs_ref, d_ref, l_ref, sf_ref, t_ref, o_ref,
    d_vm, rs_vm, x_send, x_recv, t_vm, l_vm, sw_vm, local, e_send,
    m_part, m_recv, a1, a2, a4, b1, b2, c2, a_high, a_low,
    c_part, c_recv, u_send, u_recv, v_send, v_recv, mix,
    d_sem, rs_sem, in_sem, own_sem, send_sem, recv_sem,
):
    s = lax.axis_index("slab")
    p = lax.axis_index("plane")
    tile = d_ref.shape[2]
    step = tile // CHUNKS
    side = n_plane // 2
    run = max(1, n_plane // 8)

    my_side = lax.rem(lax.div(p, run), 2)
    my_slot = lax.div(p, 2 * run) * run + lax.rem(p, run)
    far_side = 1 - my_side
    me = my_side * side + my_slot

    def place(which, i):
        return which * side + lax.rem(my_slot + i, side)

    def device_at(k):
        slot = lax.rem(k, side)
        return lax.div(slot, run) * 2 * run + lax.div(k, side) * run + lax.rem(slot, run)

    by_distance = sorted(range(side), key=lambda i: -min(i, side - i))
    far = [(k, device_at(k)) for k in (place(far_side, i) for i in by_distance)]
    near = [(k, device_at(k)) for k in (place(my_side, i) for i in by_distance if i)]

    def remote(src, dst, group, device):
        return pltpu.make_async_remote_copy(
            src_ref=src, dst_ref=dst, send_sem=send_sem.at[group], recv_sem=recv_sem.at[group],
            device_id=device, device_id_type=MESH,
        )

    peer = (s, lax.rem(p + 1, n_plane))

    def await_recv(ref, group):
        remote(ref, ref, group, peer).wait_recv()

    def await_send(ref, group):
        remote(ref, ref, group, peer).wait_send()

    others = pl.ds(0, n_plane - 1)
    near_others = pl.ds(0, side - 1)
    all_far = pl.ds(0, side)

    def to_plane(src, dst, group):
        for _, q in far + near:
            remote(src, dst, group, (s, q)).start()

    def blocks_to(targets, src, dst, group, slab):
        for k, q in targets:
            remote(src.at[k], dst, group, (slab, q)).start()

    def rs_copy(k):
        lanes = pl.ds(pl.multiple_of(device_at(k) * tile, tile), tile)
        return pltpu.make_async_copy(rs_ref.at[0, :, lanes], rs_vm.at[k], rs_sem.at[k])

    def start_rs(which):
        def one(i, carry):
            rs_copy(place(which, i)).start()
            return carry
        lax.fori_loop(0, side, one, 0)

    start_rs(my_side)
    s_copy = pltpu.make_async_copy(sf_ref.at[0], sw_vm.at[pl.ds(0, 2), pl.ds(0, rank), :], in_sem.at[1])
    s_copy.start()

    def d_copy(j):
        rows = pl.ds(pl.multiple_of(j * step, step), step)
        return pltpu.make_async_copy(d_ref.at[0, :, rows, :], d_vm.at[:, rows, :], d_sem.at[j])

    def start_d(j, carry):
        d_copy(j).start()
        return carry

    u_recv[...] = jnp.zeros_like(u_recv)
    barrier = pltpu.get_barrier_semaphore()

    def greet(device):
        pl.semaphore_signal(barrier, inc=1, device_id=device, device_id_type=MESH)

    def greet_plane(i, carry):
        greet((s, lax.rem(p + i, n_plane)))
        return carry
    lax.fori_loop(1, n_plane, greet_plane, 0)
    pl.when(s < n_slab - 1)(lambda: greet((s + 1, p)))
    for distance in (1, 2, 3, 4):
        pl.when(s >= distance)(functools.partial(lambda d: greet((s - d, p)), distance))

    start_rs(far_side)
    lax.fori_loop(0, CHUNKS, start_d, 0)
    l_copy = pltpu.make_async_copy(l_ref.at[0], l_vm.at[:, pl.ds(0, rank), :], in_sem.at[0])
    l_copy.start()
    for padded in (t_vm, l_vm, sw_vm):
        padded[pl.ds(0, 2), rank:, :] = jnp.zeros((2, PAD - rank, tile), BF16)

    a_high[...] = jnp.zeros_like(a_high)
    a_low[...] = jnp.zeros_like(a_low)

    @pl.when(s == n_slab - 1)
    def _():
        sw_vm[pl.ds(2, 4)] = jnp.zeros((4, PAD, tile), BF16)

    expected = n_plane - 1 + (s >= 1).astype(jnp.int32)
    for distance in (1, 2, 3, 4):
        expected = expected + (s + distance < n_slab).astype(jnp.int32)
    pl.semaphore_wait(barrier, expected)

    t_copy = remote(t_ref.at[0], t_vm.at[:, pl.ds(0, rank), :], T, (s - 1, p))
    pl.when(s >= 1)(t_copy.start)

    for k, q in near:
        rs_copy(k).wait()
        x_send[k] = rs_vm[k].astype(BF16)
        remote(x_send.at[k], x_recv.at[me], X0, (s, q)).start()
    rs_copy(me).wait()
    x_recv[me] = rs_vm[me].astype(BF16)

    def far_cast(i, carry):
        k = place(far_side, i)
        rs_copy(k).wait()
        x_send[k] = rs_vm[k].astype(BF16)
        return carry
    lax.fori_loop(0, side, far_cast, 0)

    def side_rows(which):
        return pl.ds(which * side, side)

    def local_part(which, begin, end, first):
        def chunk(j, carry):
            if first:
                d_copy(j).wait()
            rows = pl.ds(pl.multiple_of(j * step, step), step)
            x = x_recv[side_rows(which)].reshape(side * 16, tile)
            real = nt_dot(x, d_vm[0, rows, :])
            imag = nt_dot(x, d_vm[1, rows, :])
            local[which, :side * 8, rows] = real[:side * 8] - imag[side * 8:]
            local[which, side * 8:, rows] = real[side * 8:] + imag[:side * 8]
            return carry
        lax.fori_loop(begin, end, chunk, 0)

    def trace_weights(first, last):
        def chunk(j, carry):
            rows = pl.ds(pl.multiple_of(j * step, step), step)
            t_rows = t_vm[...].reshape(2 * PAD, tile)
            with_real = nn_dot(t_rows, d_vm[0, :, rows])
            with_imag = nn_dot(t_rows, d_vm[1, :, rows])
            for part, value in enumerate((
                with_real[:PAD] - with_imag[PAD:], with_imag[:PAD] + with_real[PAD:]
            )):
                high, low = split(value)
                sw_vm[2 + part, :, rows] = high
                sw_vm[4 + part, :, rows] = low
            return carry
        lax.fori_loop(first, last, chunk, 0)

    def rank_part(which):
        x = x_recv[side_rows(which)].reshape(side * 16, tile)
        both = nt_dot(x, sw_vm[...].reshape(6 * PAD, tile))
        source = from_products(both[:, :2 * PAD])
        trace = from_products(both[:, 2 * PAD:4 * PAD] + both[:, 4 * PAD:])
        c_part[side_rows(which), 0] = source.reshape(side, 8, 2 * PAD)
        c_part[side_rows(which), 1] = trace.reshape(side, 8, 2 * PAD)

    await_recv(x_recv.at[near_others], X0)
    local_part(my_side, 0, CHUNKS, True)
    s_copy.wait()
    l_copy.wait()

    pl.when(s >= 1)(t_copy.wait_send)

    @pl.when(s < n_slab - 1)
    def _():
        t_copy.wait_recv()
        products = nt_dot(l_vm[...].reshape(2 * PAD, tile), t_vm[...].reshape(2 * PAD, tile))
        m_part[...] = from_products(products).reshape(m_part.shape)

        blocks_to(far + near + [(me, p)], m_part, m_recv.at[me], RM, s + 1)

    first_batch = 5 * side // 8
    blocks_to(far[:first_batch], x_send, x_recv.at[me], X1, s)
    half_chunks = CHUNKS // 2
    pl.when(s < n_slab - 1)(lambda: trace_weights(0, half_chunks))

    def keep(index, top):
        high, low = split(expanded(top.reshape(PAD, 2 * PAD)))
        a_high[index] = high
        a_low[index] = low

    b1_copy = remote(a1.at[me], b1, B1, (s + 1, p))
    b2_copy = remote(a1.at[me], b2, B2, (s + 2, p))
    c2_copy = remote(a2.at[me], c2, C2, (s + 2, p))
    @pl.when(s >= 1)
    def _():
        await_recv(m_recv, RM)
        a1[me] = jnp.sum(m_recv[...], axis=0)
        to_plane(a1.at[me], a1.at[me], AM)
        pl.when(s + 1 < n_slab)(b1_copy.start)
        pl.when(s + 2 < n_slab)(b2_copy.start)

    blocks_to(far[first_batch:], x_send, x_recv.at[me], X1, s)
    pl.when(s < n_slab - 1)(lambda: trace_weights(half_chunks, CHUNKS))

    @pl.when(s >= 1)
    def _():
        await_recv(a1.at[others], AM)
        keep(0, a1[...])

    @pl.when(s >= 2)
    def _():
        await_recv(b1, B1)
        a2[me] = split_dot(b1[...], a_high[0], a_low[0])
        to_plane(a2.at[me], a2.at[me], G2)
        pl.when(s + 2 < n_slab)(c2_copy.start)

    rank_part(my_side)
    c_recv[me] = c_part[me]
    blocks_to(near, c_part, c_recv.at[me], RS, s)

    await_recv(x_recv.at[all_far], X1)
    rank_part(far_side)
    blocks_to(far, c_part, c_recv.at[me], RS, s)

    @pl.when(s >= 2)
    def _():
        await_recv(a2.at[others], G2)
        keep(1, a2[...])

    @pl.when(s >= 3)
    def _():
        await_recv(b2, B2)
        a4[me, 0] = split_dot(b2[...], a_high[1], a_low[1])
        a4[me, 1] = jnp.zeros(b2.shape, F32)

        @pl.when(s >= 4)
        def _():
            await_recv(c2, C2)
            a4[me, 1] = split_dot(c2[...], a_high[1], a_low[1])
        to_plane(a4.at[me], a4.at[me], G4)

    local_part(far_side, 0, half_chunks, False)
    await_recv(c_recv.at[others], RS)
    u_send[...] = jnp.sum(c_recv[...], axis=0)
    u_copies = []
    for index, group in enumerate((V1, V2, V3, V4)):
        copy = remote(u_send, u_recv.at[index], group, (s + index + 1, p))
        u_copies.append(copy)
        pl.when(s + index + 1 < n_slab)(copy.start)
    local_part(far_side, half_chunks, CHUNKS, False)

    @pl.when(s >= 3)
    def _():
        await_recv(a4.at[others], G4)
        keep(2, a4[:, 0])
        keep(3, a4[:, 1])

    for index in range(4):
        pl.when(s > index)(u_copies[index].wait_recv)
    total = u_send[0] + u_recv[0, 1]
    for index in range(3):
        total = total + split_dot(u_recv[index, 0] + u_recv[index + 1, 1], a_high[index], a_low[index])
    v_send[...] = total
    mix[me] = total
    v_copy = remote(v_send, v_recv, VB, (s + 4, p))
    pl.when(s + 4 < n_slab)(v_copy.start)

    @pl.when(s >= 4)
    def _():
        v_copy.wait_recv()
        mix[me] = v_send[...] + split_dot(v_recv[...], a_high[3], a_low[3])

    to_plane(mix.at[me], mix.at[me], AV)
    await_recv(mix.at[others], AV)

    mine = pl.ds(pl.multiple_of(p * tile, tile), tile)

    def solve_side(which):
        mixing = mix[side_rows(which)].reshape(side * 8, 2 * PAD)
        real, imag = mixing[:, :PAD], mixing[:, PAD:]
        square = jnp.concatenate(
            [jnp.concatenate([real, -imag], axis=1), jnp.concatenate([imag, real], axis=1)], axis=0
        )
        both = nn_dot(stacked_halves(square), l_vm[...].reshape(2 * PAD, tile))
        solved = local[which] + both[:side * 16] + both[side * 16:]
        e_send[side_rows(which)] = solved.astype(BF16).reshape(side, 16, tile)

    solve_side(far_side)
    blocks_to(far, e_send, o_ref.at[:, mine], E, s)
    solve_side(my_side)
    blocks_to(near, e_send, o_ref.at[:, mine], E, s)
    own = pltpu.make_async_copy(e_send.at[me], o_ref.at[:, mine], own_sem)
    own.start()

    await_send(x_send.at[near_others], X0)
    await_send(x_send.at[all_far], X1)
    await_send(c_part.at[others], RS)
    await_send(mix.at[others], AV)

    @pl.when(s < n_slab - 1)
    def _():
        await_send(m_part, RM)

    @pl.when(s >= 1)
    def _():
        await_send(a1.at[others], AM)
        pl.when(s + 1 < n_slab)(b1_copy.wait_send)
        pl.when(s + 2 < n_slab)(b2_copy.wait_send)

    @pl.when(s >= 2)
    def _():
        await_send(a2.at[others], G2)
        pl.when(s + 2 < n_slab)(c2_copy.wait_send)
    pl.when(s >= 3)(lambda: await_send(a4.at[others], G4))
    for index in range(4):
        pl.when(s + index + 1 < n_slab)(u_copies[index].wait_send)
    pl.when(s + 4 < n_slab)(v_copy.wait_send)
    own.wait()
    await_send(e_send.at[others], E)
    await_recv(o_ref.at[:, pl.ds(0, (n_plane - 1) * tile)], E)


def solution(mesh):
    n_slab, n_plane = mesh.shape["slab"], mesh.shape["plane"]

    def body(right_sides, diag_tiles, left_factors, source_factors, trace_factors):
        tile, rank = diag_tiles.shape[2], left_factors.shape[2]
        columns = right_sides.shape[1]
        part = PAD // n_plane
        pairs = pltpu.VMEM((n_plane, 2, 8, 2 * PAD), F32)
        ranks = pltpu.VMEM((n_plane, part, 2 * PAD), F32)
        one = pltpu.VMEM((part, 2 * PAD), F32)
        padded = pltpu.VMEM((2, PAD, tile), BF16)
        blocks = pltpu.VMEM((n_plane, columns, tile), BF16)
        squares = pltpu.VMEM((4, 2 * PAD, 2 * PAD), BF16)
        out = pl.pallas_call(
            functools.partial(kernel, n_slab, n_plane, rank),
            out_shape=jax.ShapeDtypeStruct((columns, n_plane * tile), BF16),
            in_specs=[pl.BlockSpec(memory_space=pl.ANY)] * 5,
            out_specs=pl.BlockSpec(memory_space=pl.ANY),
            scratch_shapes=[
                pltpu.VMEM((2, tile, tile), BF16),
                pltpu.VMEM((n_plane, columns, tile), F32),
                blocks, blocks, padded, padded, pltpu.VMEM((6, PAD, tile), BF16),
                pltpu.VMEM((2, columns * n_plane // 2, tile), F32),
                blocks,
                ranks, ranks, ranks, ranks, pltpu.VMEM((n_plane, 2, part, 2 * PAD), F32),
                one, one, one, squares, squares,
                pairs, pairs,
                pltpu.VMEM((2, 8, 2 * PAD), F32),
                pltpu.VMEM((4, 2, 8, 2 * PAD), F32),
                pltpu.VMEM((8, 2 * PAD), F32),
                pltpu.VMEM((8, 2 * PAD), F32),
                pltpu.VMEM((n_plane, 8, 2 * PAD), F32),
                pltpu.SemaphoreType.DMA((CHUNKS,)),
                pltpu.SemaphoreType.DMA((n_plane,)),
                pltpu.SemaphoreType.DMA((2,)),
                pltpu.SemaphoreType.DMA,
                pltpu.SemaphoreType.DMA((N_GROUPS,)),
                pltpu.SemaphoreType.DMA((N_GROUPS,)),
            ],
            compiler_params=pltpu.CompilerParams(
                collective_id=0, has_side_effects=True, vmem_limit_bytes=60 * 2**20
            ),
            name="sweep",
        )(right_sides, diag_tiles, left_factors, source_factors, trace_factors)
        return out.astype(F32)[None]

    placed = (
        P("slab", "plane", None),
        P("slab", None, "plane", None),
        P("slab", None, None, "plane"),
        P("slab", None, None, "plane"),
        P("slab", None, None, "plane"),
    )
    return jax.shard_map(
        body, mesh=mesh, in_specs=placed, out_specs=P("slab", "plane", None), check_vma=False
    )
```

```python
import functools

import jax
import jax.numpy as jnp
from jax import lax
from jax.experimental import pallas as pl
from jax.experimental.pallas import tpu as pltpu
from jax.sharding import PartitionSpec as P

MESH = pl.DeviceIdType.MESH
F32 = jnp.float32
BF16 = jnp.bfloat16
PAD = 128
CHUNKS = 8
X0, X1, T, RM, AM, B1, B2, C2, G2, G4, RS, V1, V2, V3, V4, VB, AV, E = range(18)
N_GROUPS = 18
FIRST, SECOND = 3, 5
PLAN = (3, 2)
EARLY_COMPOSITE = False


def split(value):
    high = value.astype(BF16)
    low = (value - high.astype(F32)).astype(BF16)
    return high, low


def nt_dot(rows, mat):
    return lax.dot_general(rows, mat, (((1,), (1,)), ((), ())), preferred_element_type=F32)


def nn_dot(rows, mat):
    return lax.dot_general(rows, mat, (((1,), (0,)), ((), ())), preferred_element_type=F32)


def from_products(both):
    half = both.shape[0] // 2
    real = both[:half, :PAD] - both[half:, PAD:]
    imag = both[half:, :PAD] + both[:half, PAD:]
    return jnp.concatenate([real, imag], axis=1)


def expanded(top):
    real, imag = top[:, :PAD], top[:, PAD:]
    return jnp.concatenate([top, jnp.concatenate([-imag, real], axis=1)], axis=0)


def stacked_halves(rows):
    rows_high = rows.astype(BF16).astype(F32)
    return jnp.concatenate([rows_high, rows - rows_high], axis=0).astype(BF16)


def split_dot(rows, high, low):
    count = rows.shape[0]
    stacked = stacked_halves(rows)
    total = nn_dot(stacked, high) + nn_dot(stacked, low)
    return total[:count] + total[count:]


def kernel(
    n_slab, n_plane, rank,
    rs_ref, d_ref, l_ref, sf_ref, t_ref, o_ref,
    d_vm, rs_vm, x_send, x_recv, t_vm, l_vm, sw_vm, local, e_send,
    m_part, m_recv, a1, a2, a4, b1, b2, c2, a_high, a_low,
    c_part, c_recv, u_send, u_recv, v_send, v_recv, mix,
    d_sem, rs_sem, in_sem, own_sem, send_sem, recv_sem,
):
    s = lax.axis_index("slab")
    p = lax.axis_index("plane")
    tile = d_ref.shape[2]
    step = tile // CHUNKS
    side = n_plane // 2
    run = max(1, n_plane // 8)

    my_side = lax.rem(lax.div(p, run), 2)
    my_slot = lax.div(p, 2 * run) * run + lax.rem(p, run)
    far_side = 1 - my_side
    me = my_side * side + my_slot

    def place(which, i):
        return which * side + lax.rem(my_slot + i, side)

    def device_at(k):
        slot = lax.rem(k, side)
        return lax.div(slot, run) * 2 * run + lax.div(k, side) * run + lax.rem(slot, run)

    by_distance = sorted(range(side), key=lambda i: -min(i, side - i))
    far = [(k, device_at(k)) for k in (place(far_side, i) for i in by_distance)]
    near = [(k, device_at(k)) for k in (place(my_side, i) for i in by_distance if i)]

    def remote(src, dst, group, device):
        return pltpu.make_async_remote_copy(
            src_ref=src, dst_ref=dst, send_sem=send_sem.at[group], recv_sem=recv_sem.at[group],
            device_id=device, device_id_type=MESH,
        )

    peer = (s, lax.rem(p + 1, n_plane))

    def await_recv(ref, group):
        remote(ref, ref, group, peer).wait_recv()

    def await_send(ref, group):
        remote(ref, ref, group, peer).wait_send()

    others = pl.ds(0, n_plane - 1)
    near_others = pl.ds(0, side - 1)
    all_far = pl.ds(0, side)

    def to_plane(src, dst, group):
        for _, q in far + near:
            remote(src, dst, group, (s, q)).start()

    def blocks_to(targets, src, dst, group, slab):
        for k, q in targets:
            remote(src.at[k], dst, group, (slab, q)).start()

    u_recv[...] = jnp.zeros_like(u_recv)
    barrier = pltpu.get_barrier_semaphore()

    def greet(device):
        pl.semaphore_signal(barrier, inc=1, device_id=device, device_id_type=MESH)

    def greet_plane(i, carry):
        greet((s, lax.rem(p + i, n_plane)))
        return carry
    lax.fori_loop(1, n_plane, greet_plane, 0)
    pl.when(s < n_slab - 1)(lambda: greet((s + 1, p)))
    for distance in (1, 2, 3, 4):
        pl.when(s >= distance)(functools.partial(lambda d: greet((s - d, p)), distance))


    def rs_copy(k):
        lanes = pl.ds(pl.multiple_of(device_at(k) * tile, tile), tile)
        return pltpu.make_async_copy(rs_ref.at[0, :, lanes], rs_vm.at[k], rs_sem.at[k])

    def start_rs(which):
        def one(i, carry):
            rs_copy(place(which, i)).start()
            return carry
        lax.fori_loop(0, side, one, 0)

    start_rs(my_side)
    s_copy = pltpu.make_async_copy(sf_ref.at[0], sw_vm.at[pl.ds(0, 2), pl.ds(0, rank), :], in_sem.at[1])
    s_copy.start()

    def d_copy(j):
        rows = pl.ds(pl.multiple_of(j * step, step), step)
        return pltpu.make_async_copy(d_ref.at[0, :, rows, :], d_vm.at[:, rows, :], d_sem.at[j])

    def start_d(j, carry):
        d_copy(j).start()
        return carry

    start_rs(far_side)
    lax.fori_loop(0, CHUNKS, start_d, 0)
    l_copy = pltpu.make_async_copy(l_ref.at[0], l_vm.at[:, pl.ds(0, rank), :], in_sem.at[0])
    l_copy.start()
    for padded in (t_vm, l_vm, sw_vm):
        padded[pl.ds(0, 2), rank:, :] = jnp.zeros((2, PAD - rank, tile), BF16)

    a_high[...] = jnp.zeros_like(a_high)
    a_low[...] = jnp.zeros_like(a_low)

    @pl.when(s == n_slab - 1)
    def _():
        sw_vm[pl.ds(2, 4)] = jnp.zeros((4, PAD, tile), BF16)

    expected = n_plane - 1 + (s >= 1).astype(jnp.int32)
    for distance in (1, 2, 3, 4):
        expected = expected + (s + distance < n_slab).astype(jnp.int32)
    pl.semaphore_wait(barrier, expected)

    t_copy = remote(t_ref.at[0], t_vm.at[:, pl.ds(0, rank), :], T, (s - 1, p))
    pl.when(s >= 1)(t_copy.start)

    for k, q in near:
        rs_copy(k).wait()
        x_send[k] = rs_vm[k].astype(BF16)
        remote(x_send.at[k], x_recv.at[me], X0, (s, q)).start()
    rs_copy(me).wait()
    x_recv[me] = rs_vm[me].astype(BF16)

    def far_cast(i, carry):
        k = place(far_side, i)
        rs_copy(k).wait()
        x_send[k] = rs_vm[k].astype(BF16)
        return carry
    lax.fori_loop(0, side, far_cast, 0)

    def side_rows(which):
        return pl.ds(which * side, side)

    def local_part(which, begin, end, first):
        def chunk(j, carry):
            if first:
                d_copy(j).wait()
            rows = pl.ds(pl.multiple_of(j * step, step), step)
            x = x_recv[side_rows(which)].reshape(side * 16, tile)
            real = nt_dot(x, d_vm[0, rows, :])
            imag = nt_dot(x, d_vm[1, rows, :])
            local[which, :side * 8, rows] = real[:side * 8] - imag[side * 8:]
            local[which, side * 8:, rows] = real[side * 8:] + imag[:side * 8]
            return carry
        lax.fori_loop(begin, end, chunk, 0)

    def trace_weights(first, last):
        def chunk(j, carry):
            rows = pl.ds(pl.multiple_of(j * step, step), step)
            t_rows = t_vm[...].reshape(2 * PAD, tile)
            with_real = nn_dot(t_rows, d_vm[0, :, rows])
            with_imag = nn_dot(t_rows, d_vm[1, :, rows])
            for part, value in enumerate((
                with_real[:PAD] - with_imag[PAD:], with_imag[:PAD] + with_real[PAD:]
            )):
                high, low = split(value)
                sw_vm[2 + part, :, rows] = high
                sw_vm[4 + part, :, rows] = low
            return carry
        lax.fori_loop(first, last, chunk, 0)

    def rank_part(which):
        x = x_recv[side_rows(which)].reshape(side * 16, tile)
        both = nt_dot(x, sw_vm[...].reshape(6 * PAD, tile))
        source = from_products(both[:, :2 * PAD])
        trace = from_products(both[:, 2 * PAD:4 * PAD] + both[:, 4 * PAD:])
        c_part[side_rows(which), 0] = source.reshape(side, 8, 2 * PAD)
        c_part[side_rows(which), 1] = trace.reshape(side, 8, 2 * PAD)

    await_recv(x_recv.at[near_others], X0)
    local_part(my_side, 0, CHUNKS, True)
    s_copy.wait()
    l_copy.wait()

    first, second = FIRST * side // 8, SECOND * side // 8
    pl.when(s >= 1)(t_copy.wait_send)
    blocks_to(far[:first], x_send, x_recv.at[me], X1, s)

    @pl.when(s < n_slab - 1)
    def _():
        t_copy.wait_recv()
        products = nt_dot(l_vm[...].reshape(2 * PAD, tile), t_vm[...].reshape(2 * PAD, tile))
        m_part[...] = from_products(products).reshape(m_part.shape)

        blocks_to(far + near + [(me, p)], m_part, m_recv.at[me], RM, s + 1)

    blocks_to(far[first:second], x_send, x_recv.at[me], X1, s)
    half_chunks = CHUNKS // 2
    pl.when(s < n_slab - 1)(lambda: trace_weights(0, half_chunks))

    def keep(index, top):
        high, low = split(expanded(top.reshape(PAD, 2 * PAD)))
        a_high[index] = high
        a_low[index] = low

    b1_copy = remote(a1.at[me], b1, B1, (s + 1, p))
    b2_copy = remote(a1.at[me], b2, B2, (s + 2, p))
    c2_copy = remote(a2.at[me], c2, C2, (s + 2, p))
    @pl.when(s >= 1)
    def _():
        await_recv(m_recv, RM)
        a1[me] = jnp.sum(m_recv[...], axis=0)
        to_plane(a1.at[me], a1.at[me], AM)
        pl.when(s + 1 < n_slab)(b1_copy.start)
        pl.when(s + 2 < n_slab)(b2_copy.start)

    blocks_to(far[second:], x_send, x_recv.at[me], X1, s)
    pl.when(s < n_slab - 1)(lambda: trace_weights(half_chunks, CHUNKS))

    rank_part(my_side)
    c_recv[me] = c_part[me]
    blocks_to(near, c_part, c_recv.at[me], RS, s)

    @pl.when(s >= 1)
    def _():
        await_recv(a1.at[others], AM)
        keep(0, a1[...])

    @pl.when(s >= 2)
    def _():
        await_recv(b1, B1)
        a2[me] = split_dot(b1[...], a_high[0], a_low[0])
        to_plane(a2.at[me], a2.at[me], G2)
        pl.when(s + 2 < n_slab)(c2_copy.start)

    def longer_composites():
        @pl.when(s >= 2)
        def _():
            await_recv(a2.at[others], G2)
            keep(1, a2[...])

        @pl.when(s >= 3)
        def _():
            await_recv(b2, B2)
            a4[me, 0] = split_dot(b2[...], a_high[1], a_low[1])
            a4[me, 1] = jnp.zeros(b2.shape, F32)

            @pl.when(s >= 4)
            def _():
                await_recv(c2, C2)
                a4[me, 1] = split_dot(c2[...], a_high[1], a_low[1])
            to_plane(a4.at[me], a4.at[me], G4)

    if EARLY_COMPOSITE:
        longer_composites()

    await_recv(x_recv.at[all_far], X1)
    rank_part(far_side)
    blocks_to(far, c_part, c_recv.at[me], RS, s)

    if not EARLY_COMPOSITE:
        longer_composites()

    before_sums, before_scan = PLAN[0], PLAN[0] + PLAN[1]
    local_part(far_side, 0, before_sums, False)
    await_recv(c_recv.at[others], RS)
    u_send[...] = jnp.sum(c_recv[...], axis=0)
    u_copies = []
    for index, group in enumerate((V1, V2, V3, V4)):
        copy = remote(u_send, u_recv.at[index], group, (s + index + 1, p))
        u_copies.append(copy)
        pl.when(s + index + 1 < n_slab)(copy.start)
    local_part(far_side, before_sums, before_scan, False)

    @pl.when(s >= 3)
    def _():
        await_recv(a4.at[others], G4)
        keep(2, a4[:, 0])
        keep(3, a4[:, 1])

    for index in range(4):
        pl.when(s > index)(u_copies[index].wait_recv)
    total = u_send[0] + u_recv[0, 1]
    for index in range(3):
        total = total + split_dot(u_recv[index, 0] + u_recv[index + 1, 1], a_high[index], a_low[index])
    v_send[...] = total
    mix[me] = total
    v_copy = remote(v_send, v_recv, VB, (s + 4, p))
    pl.when(s + 4 < n_slab)(v_copy.start)

    @pl.when(s >= 4)
    def _():
        v_copy.wait_recv()
        mix[me] = v_send[...] + split_dot(v_recv[...], a_high[3], a_low[3])

    to_plane(mix.at[me], mix.at[me], AV)
    local_part(far_side, before_scan, CHUNKS, False)
    await_recv(mix.at[others], AV)

    mine = pl.ds(pl.multiple_of(p * tile, tile), tile)

    def solve_side(which):
        mixing = mix[side_rows(which)].reshape(side * 8, 2 * PAD)
        real, imag = mixing[:, :PAD], mixing[:, PAD:]
        square = jnp.concatenate(
            [jnp.concatenate([real, -imag], axis=1), jnp.concatenate([imag, real], axis=1)], axis=0
        )
        both = nn_dot(stacked_halves(square), l_vm[...].reshape(2 * PAD, tile))
        solved = local[which] + both[:side * 16] + both[side * 16:]
        e_send[side_rows(which)] = solved.astype(BF16).reshape(side, 16, tile)

    solve_side(far_side)
    blocks_to(far, e_send, o_ref.at[:, mine], E, s)
    solve_side(my_side)
    blocks_to(near, e_send, o_ref.at[:, mine], E, s)
    own = pltpu.make_async_copy(e_send.at[me], o_ref.at[:, mine], own_sem)
    own.start()

    await_send(x_send.at[near_others], X0)
    await_send(x_send.at[all_far], X1)
    await_send(c_part.at[others], RS)
    await_send(mix.at[others], AV)

    @pl.when(s < n_slab - 1)
    def _():
        await_send(m_part, RM)

    @pl.when(s >= 1)
    def _():
        await_send(a1.at[others], AM)
        pl.when(s + 1 < n_slab)(b1_copy.wait_send)
        pl.when(s + 2 < n_slab)(b2_copy.wait_send)

    @pl.when(s >= 2)
    def _():
        await_send(a2.at[others], G2)
        pl.when(s + 2 < n_slab)(c2_copy.wait_send)
    pl.when(s >= 3)(lambda: await_send(a4.at[others], G4))
    for index in range(4):
        pl.when(s + index + 1 < n_slab)(u_copies[index].wait_send)
    pl.when(s + 4 < n_slab)(v_copy.wait_send)
    own.wait()
    await_send(e_send.at[others], E)
    await_recv(o_ref.at[:, pl.ds(0, (n_plane - 1) * tile)], E)


def solution(mesh):
    n_slab, n_plane = mesh.shape["slab"], mesh.shape["plane"]

    def body(right_sides, diag_tiles, left_factors, source_factors, trace_factors):
        tile, rank = diag_tiles.shape[2], left_factors.shape[2]
        columns = right_sides.shape[1]
        part = PAD // n_plane
        pairs = pltpu.VMEM((n_plane, 2, 8, 2 * PAD), F32)
        ranks = pltpu.VMEM((n_plane, part, 2 * PAD), F32)
        one = pltpu.VMEM((part, 2 * PAD), F32)
        padded = pltpu.VMEM((2, PAD, tile), BF16)
        blocks = pltpu.VMEM((n_plane, columns, tile), BF16)
        squares = pltpu.VMEM((4, 2 * PAD, 2 * PAD), BF16)
        out = pl.pallas_call(
            functools.partial(kernel, n_slab, n_plane, rank),
            out_shape=jax.ShapeDtypeStruct((columns, n_plane * tile), BF16),
            in_specs=[pl.BlockSpec(memory_space=pl.ANY)] * 5,
            out_specs=pl.BlockSpec(memory_space=pl.ANY),
            scratch_shapes=[
                pltpu.VMEM((2, tile, tile), BF16),
                pltpu.VMEM((n_plane, columns, tile), F32),
                blocks, blocks, padded, padded, pltpu.VMEM((6, PAD, tile), BF16),
                pltpu.VMEM((2, columns * n_plane // 2, tile), F32),
                blocks,
                ranks, ranks, ranks, ranks, pltpu.VMEM((n_plane, 2, part, 2 * PAD), F32),
                one, one, one, squares, squares,
                pairs, pairs,
                pltpu.VMEM((2, 8, 2 * PAD), F32),
                pltpu.VMEM((4, 2, 8, 2 * PAD), F32),
                pltpu.VMEM((8, 2 * PAD), F32),
                pltpu.VMEM((8, 2 * PAD), F32),
                pltpu.VMEM((n_plane, 8, 2 * PAD), F32),
                pltpu.SemaphoreType.DMA((CHUNKS,)),
                pltpu.SemaphoreType.DMA((n_plane,)),
                pltpu.SemaphoreType.DMA((2,)),
                pltpu.SemaphoreType.DMA,
                pltpu.SemaphoreType.DMA((N_GROUPS,)),
                pltpu.SemaphoreType.DMA((N_GROUPS,)),
            ],
            compiler_params=pltpu.CompilerParams(
                collective_id=0, has_side_effects=True, vmem_limit_bytes=60 * 2**20
            ),
            name="sweep",
        )(right_sides, diag_tiles, left_factors, source_factors, trace_factors)
        return out.astype(F32)[None]

    placed = (
        P("slab", "plane", None),
        P("slab", None, "plane", None),
        P("slab", None, None, "plane"),
        P("slab", None, None, "plane"),
        P("slab", None, None, "plane"),
    )
    return jax.shard_map(
        body, mesh=mesh, in_specs=placed, out_specs=P("slab", "plane", None), check_vma=False
    )
```

```python
import functools

import jax
import jax.numpy as jnp
from jax import lax
from jax.experimental import pallas as pl
from jax.experimental.pallas import tpu as pltpu
from jax.sharding import PartitionSpec as P

MESH = pl.DeviceIdType.MESH
F32 = jnp.float32
BF16 = jnp.bfloat16
PAD = 128
CHUNKS = 8
X0, X1, T, RM, AM, RS, AV, E, U, MH, MS = 0, 1, 2, 3, 4, 5, 6, 7, 8, 15, 22
N_GROUPS = 29
FIRST = 5
PLAN = (2, 3)


def split(value):
    high = value.astype(BF16)
    low = (value - high.astype(F32)).astype(BF16)
    return high, low


def nt_dot(rows, mat):
    return lax.dot_general(rows, mat, (((1,), (1,)), ((), ())), preferred_element_type=F32)


def nn_dot(rows, mat):
    return lax.dot_general(rows, mat, (((1,), (0,)), ((), ())), preferred_element_type=F32)


def from_products(both):
    half = both.shape[0] // 2
    real = both[:half, :PAD] - both[half:, PAD:]
    imag = both[half:, :PAD] + both[:half, PAD:]
    return jnp.concatenate([real, imag], axis=1)


def moved(rows, *parts):
    count = rows.shape[0]
    upright = jnp.concatenate([rows[:, :PAD], rows[:, PAD:]], axis=0)
    stacked = stacked_halves(upright)
    both = sum(nn_dot(stacked, part) for part in parts)
    both = both[:2 * count] + both[2 * count:]
    return from_products(both)


def stacked_halves(rows):
    rows_high = rows.astype(BF16).astype(F32)
    return jnp.concatenate([rows_high, rows - rows_high], axis=0).astype(BF16)


def kernel(
    n_slab, n_plane, rank,
    rs_ref, d_ref, l_ref, sf_ref, t_ref, o_ref,
    d_vm, rs_vm, x_send, x_recv, t_vm, l_vm, sw_vm, local, e_send,
    m_part, m_recv, a1, earlier,
    c_part, c_recv, u_send, u_recv, mix,
    d_sem, rs_sem, in_sem, own_sem, send_sem, recv_sem,
):
    s = lax.axis_index("slab")
    p = lax.axis_index("plane")
    tile = d_ref.shape[2]
    step = tile // CHUNKS
    side = n_plane // 2
    run = max(1, n_plane // 8)

    my_side = lax.rem(lax.div(p, run), 2)
    my_slot = lax.div(p, 2 * run) * run + lax.rem(p, run)
    far_side = 1 - my_side
    me = my_side * side + my_slot

    def place(which, i):
        return which * side + lax.rem(my_slot + i, side)

    def device_at(k):
        slot = lax.rem(k, side)
        return lax.div(slot, run) * 2 * run + lax.div(k, side) * run + lax.rem(slot, run)

    by_distance = sorted(range(side), key=lambda i: -min(i, side - i))
    far = [(k, device_at(k)) for k in (place(far_side, i) for i in by_distance)]
    near = [(k, device_at(k)) for k in (place(my_side, i) for i in by_distance if i)]

    def remote(src, dst, group, device):
        return pltpu.make_async_remote_copy(
            src_ref=src, dst_ref=dst, send_sem=send_sem.at[group], recv_sem=recv_sem.at[group],
            device_id=device, device_id_type=MESH,
        )

    peer = (s, lax.rem(p + 1, n_plane))

    def await_recv(ref, group):
        remote(ref, ref, group, peer).wait_recv()

    def await_send(ref, group):
        remote(ref, ref, group, peer).wait_send()

    others = pl.ds(0, n_plane - 1)
    held = m_part.shape[1]
    n_owners = rank // held
    spread = [2 * i for i in range(3)] + [side + 2 * i for i in range(1, 4)]
    owner_places = spread if n_plane == 16 else list(range(n_owners))
    owner_devices = [(k % side) // run * 2 * run + k // side * run + k % side % run for k in owner_places]
    owner, my_rows = me < 0, jnp.int32(0)
    for j, k in enumerate(owner_places):
        owner = owner | (me == k)
        my_rows = my_rows + j * (me == k).astype(jnp.int32)
    all_rows = pl.ds(0, n_owners)
    near_others = pl.ds(0, side - 1)
    all_far = pl.ds(0, side)

    def to_plane(src, dst, group):
        for _, q in far + near:
            remote(src, dst, group, (s, q)).start()

    def blocks_to(targets, src, dst, group, slab):
        for k, q in targets:
            remote(src.at[k], dst, group, (slab, q)).start()

    for slot in range(2):
        a1[slot, n_owners:] = jnp.zeros(a1.shape[1:], BF16)[n_owners:]
    for slot in range(n_slab - 1):
        for part in range(2):
            earlier[slot, part, n_owners:] = jnp.zeros(a1.shape[1:], BF16)[n_owners:]
    barrier = pltpu.get_barrier_semaphore()

    def greet(device):
        pl.semaphore_signal(barrier, inc=1, device_id=device, device_id_type=MESH)

    def greet_plane(i, carry):
        greet((s, lax.rem(p + i, n_plane)))
        return carry
    lax.fori_loop(1, n_plane, greet_plane, 0)
    pl.when(s < n_slab - 1)(lambda: greet((s + 1, p)))
    for distance in range(1, n_slab):
        pl.when(s >= distance)(functools.partial(lambda d: greet((s - d, p)), distance))


    def rs_copy(k):
        lanes = pl.ds(pl.multiple_of(device_at(k) * tile, tile), tile)
        return pltpu.make_async_copy(rs_ref.at[0, :, lanes], rs_vm.at[k], rs_sem.at[k])

    def start_rs(which):
        def one(i, carry):
            rs_copy(place(which, i)).start()
            return carry
        lax.fori_loop(0, side, one, 0)

    start_rs(my_side)
    s_copy = pltpu.make_async_copy(sf_ref.at[0], sw_vm.at[pl.ds(0, 2), pl.ds(0, rank), :], in_sem.at[1])
    s_copy.start()

    def d_copy(j):
        rows = pl.ds(pl.multiple_of(j * step, step), step)
        return pltpu.make_async_copy(d_ref.at[0, :, rows, :], d_vm.at[:, rows, :], d_sem.at[j])

    def start_d(j, carry):
        d_copy(j).start()
        return carry

    start_rs(far_side)
    lax.fori_loop(0, CHUNKS, start_d, 0)
    l_copy = pltpu.make_async_copy(l_ref.at[0], l_vm.at[:, pl.ds(0, rank), :], in_sem.at[0])
    l_copy.start()
    for padded in (t_vm, l_vm, sw_vm):
        padded[pl.ds(0, 2), rank:, :] = jnp.zeros((2, PAD - rank, tile), BF16)


    @pl.when(s == n_slab - 1)
    def _():
        sw_vm[pl.ds(2, 4)] = jnp.zeros((4, PAD, tile), BF16)

    expected = n_plane - 1 + (s >= 1).astype(jnp.int32)
    for distance in range(1, n_slab):
        expected = expected + (s + distance < n_slab).astype(jnp.int32)
    pl.semaphore_wait(barrier, expected)

    t_copy = remote(t_ref.at[0], t_vm.at[:, pl.ds(0, rank), :], T, (s - 1, p))
    pl.when(s >= 1)(t_copy.start)

    for k, q in near:
        rs_copy(k).wait()
        x_send[k] = rs_vm[k].astype(BF16)
        remote(x_send.at[k], x_recv.at[me], X0, (s, q)).start()
    rs_copy(me).wait()
    x_recv[me] = rs_vm[me].astype(BF16)

    def far_cast(i, carry):
        k = place(far_side, i)
        rs_copy(k).wait()
        x_send[k] = rs_vm[k].astype(BF16)
        return carry
    lax.fori_loop(0, side, far_cast, 0)

    def side_rows(which):
        return pl.ds(which * side, side)

    def local_part(which, begin, end, first):
        def chunk(j, carry):
            if first:
                d_copy(j).wait()
            rows = pl.ds(pl.multiple_of(j * step, step), step)
            x = x_recv[side_rows(which)].reshape(side * 16, tile)
            real = nt_dot(d_vm[0, rows, :], x).T
            imag = nt_dot(d_vm[1, rows, :], x).T
            local[which, :side * 8, rows] = real[:side * 8] - imag[side * 8:]
            local[which, side * 8:, rows] = real[side * 8:] + imag[:side * 8]
            return carry
        lax.fori_loop(begin, end, chunk, 0)

    def trace_weights(first, last):
        def chunk(j, carry):
            rows = pl.ds(pl.multiple_of(j * step, step), step)
            t_rows = t_vm[...].reshape(2 * PAD, tile)
            with_real = nn_dot(t_rows, d_vm[0, :, rows])
            with_imag = nn_dot(t_rows, d_vm[1, :, rows])
            for part, value in enumerate((
                with_real[:PAD] - with_imag[PAD:], with_imag[:PAD] + with_real[PAD:]
            )):
                high, low = split(value)
                sw_vm[2 + part, :, rows] = high
                sw_vm[4 + part, :, rows] = low
            return carry
        lax.fori_loop(first, last, chunk, 0)

    def rank_part(which):
        x = x_recv[side_rows(which)].reshape(side * 16, tile)
        both = nt_dot(x, sw_vm[...].reshape(6 * PAD, tile))
        source = from_products(both[:, :2 * PAD])
        trace = from_products(both[:, 2 * PAD:4 * PAD] + both[:, 4 * PAD:])
        c_part[side_rows(which), 0] = source.reshape(side, 8, 2 * PAD)
        c_part[side_rows(which), 1] = trace.reshape(side, 8, 2 * PAD)

    await_recv(x_recv.at[near_others], X0)
    local_part(my_side, 0, CHUNKS, True)
    s_copy.wait()
    l_copy.wait()

    first = FIRST * side // 8
    pl.when(s >= 1)(t_copy.wait_send)
    blocks_to(far[:first], x_send, x_recv.at[me], X1, s)

    @pl.when(s < n_slab - 1)
    def _():
        t_copy.wait_recv()
        products = nt_dot(l_vm[...].reshape(2 * PAD, tile), t_vm[...].reshape(2 * PAD, tile))
        m_part[...] = from_products(products).reshape(m_part.shape)

        for j, q in enumerate(owner_devices):
            remote(m_part.at[j], m_recv.at[me], RM, (s + 1, q)).start()

    blocks_to(far[first:], x_send, x_recv.at[me], X1, s)
    pl.when(s < n_slab - 1)(lambda: trace_weights(0, CHUNKS))

    @pl.when((s >= 1) & owner)
    def _():
        await_recv(m_recv, RM)
        high, low = split(jnp.sum(m_recv[...], axis=0))
        a1[0, my_rows] = high
        a1[1, my_rows] = low
        to_plane(a1.at[:, my_rows], a1.at[:, my_rows], AM)

    rank_part(my_side)
    c_recv[me] = c_part[me]
    blocks_to(near, c_part, c_recv.at[me], RS, s)

    part = lax.rem(p, 2)
    partner = (s, p + 1 - 2 * part)
    later_copies = [
        (
            remote(a1.at[part, all_rows], earlier.at[d - 1, part, all_rows], MH + d - 1, (s + d, p)),
            (s >= 1) & (s + d < n_slab),
        )
        for d in range(1, n_slab)
    ]
    shared_copies = [
        remote(earlier.at[d - 1, part, all_rows], earlier.at[d - 1, part, all_rows], MS + d - 1, partner)
        for d in range(1, n_slab)
    ]

    def send_later():
        @pl.when(s >= 1)
        def _():
            pl.when(owner)(lambda: await_recv(a1.at[:, pl.ds(0, n_owners - 1)], AM))
            pl.when(jnp.logical_not(owner))(lambda: await_recv(a1.at[:, all_rows], AM))
            for copy, needed in later_copies:
                pl.when(needed)(copy.start)

    await_recv(x_recv.at[all_far], X1)
    rank_part(far_side)
    blocks_to(far, c_part, c_recv.at[me], RS, s)

    send_later()

    before_sums, before_scan = PLAN[0], PLAN[0] + PLAN[1]
    local_part(far_side, 0, before_sums, False)
    await_recv(c_recv.at[others], RS)
    u_send[...] = jnp.sum(c_recv[...], axis=0)
    u_copies = []
    for distance in range(1, n_slab):
        copy = remote(u_send, u_recv.at[distance - 1], U + distance - 1, (s + distance, p))
        u_copies.append(copy)
        pl.when(s + distance < n_slab)(copy.start)
    local_part(far_side, before_sums, before_scan, False)
    for d in range(1, n_slab - 1):
        @pl.when(s > d)
        def _():
            later_copies[d - 1][0].wait_recv()
            shared_copies[d - 1].start()

    def await_u(distance):
        remote(u_send, u_recv.at[0], U + distance - 1, peer).wait_recv()

    mix[me] = u_send[0]

    @pl.when(s >= 1)
    def _():
        await_u(s)

        def advance(step_back, value):
            d = s - step_back
            await_u(d)
            remote(a1.at[0, all_rows], earlier.at[0, 0, all_rows], MS + d - 1, peer).wait_recv()
            high, low = earlier[d - 1, 0].reshape(PAD, 2 * PAD), earlier[d - 1, 1].reshape(PAD, 2 * PAD)
            return u_recv[d - 1, 0] + u_recv[d, 1] + moved(value, high, low)
        value = lax.fori_loop(1, s, advance, u_recv[s - 1, 0])
        high, low = a1[0].reshape(PAD, 2 * PAD), a1[1].reshape(PAD, 2 * PAD)
        mix[me] = u_send[0] + u_recv[0, 1] + moved(value, high, low)

    to_plane(mix.at[me], mix.at[me], AV)
    local_part(far_side, before_scan, CHUNKS, False)
    await_recv(mix.at[others], AV)

    mine = pl.ds(pl.multiple_of(p * tile, tile), tile)

    def solve_side(which):
        mixing = mix[side_rows(which)].reshape(side * 8, 2 * PAD)
        real, imag = mixing[:, :PAD], mixing[:, PAD:]
        square = jnp.concatenate(
            [jnp.concatenate([real, -imag], axis=1), jnp.concatenate([imag, real], axis=1)], axis=0
        )
        both = nn_dot(stacked_halves(square), l_vm[...].reshape(2 * PAD, tile))
        solved = local[which] + both[:side * 16] + both[side * 16:]
        e_send[side_rows(which)] = solved.astype(BF16).reshape(side, 16, tile)

    solve_side(far_side)
    blocks_to(far, e_send, o_ref.at[:, mine], E, s)
    solve_side(my_side)
    blocks_to(near, e_send, o_ref.at[:, mine], E, s)
    own = pltpu.make_async_copy(e_send.at[me], o_ref.at[:, mine], own_sem)
    own.start()

    await_send(x_send.at[near_others], X0)
    await_send(x_send.at[all_far], X1)
    await_send(c_part.at[others], RS)
    await_send(mix.at[others], AV)

    @pl.when(s < n_slab - 1)
    def _():
        await_send(m_part.at[all_rows], RM)

    pl.when((s >= 1) & owner)(lambda: await_send(m_recv.at[others], AM))
    for copy, needed in later_copies:
        pl.when(needed)(copy.wait_send)
    for d in range(1, n_slab - 1):
        pl.when(s > d)(shared_copies[d - 1].wait_send)
    for distance in range(1, n_slab):
        pl.when(s + distance < n_slab)(u_copies[distance - 1].wait_send)
    own.wait()
    await_send(e_send.at[others], E)
    await_recv(o_ref.at[:, pl.ds(0, (n_plane - 1) * tile)], E)


def solution(mesh):
    n_slab, n_plane = mesh.shape["slab"], mesh.shape["plane"]

    def body(right_sides, diag_tiles, left_factors, source_factors, trace_factors):
        tile, rank = diag_tiles.shape[2], left_factors.shape[2]
        columns = right_sides.shape[1]
        held = 16 if n_plane == 16 else 32
        pairs = pltpu.VMEM((n_plane, 2, 8, 2 * PAD), F32)
        padded = pltpu.VMEM((2, PAD, tile), BF16)
        blocks = pltpu.VMEM((n_plane, columns, tile), BF16)
        out = pl.pallas_call(
            functools.partial(kernel, n_slab, n_plane, rank),
            out_shape=jax.ShapeDtypeStruct((columns, n_plane * tile), BF16),
            in_specs=[pl.BlockSpec(memory_space=pl.ANY)] * 5,
            out_specs=pl.BlockSpec(memory_space=pl.ANY),
            scratch_shapes=[
                pltpu.VMEM((2, tile, tile), BF16),
                pltpu.VMEM((n_plane, columns, tile), F32),
                blocks, blocks, padded, padded, pltpu.VMEM((6, PAD, tile), BF16),
                pltpu.VMEM((2, columns * n_plane // 2, tile), F32),
                blocks,
                pltpu.VMEM((PAD // held, held, 2 * PAD), F32),
                pltpu.VMEM((n_plane, held, 2 * PAD), F32),
                pltpu.VMEM((2, PAD // held, held, 2 * PAD), BF16),
                pltpu.VMEM((n_slab - 1, 2, PAD // held, held, 2 * PAD), BF16),
                pairs, pairs,
                pltpu.VMEM((2, 8, 2 * PAD), F32),
                pltpu.VMEM((n_slab - 1, 2, 8, 2 * PAD), F32),
                pltpu.VMEM((n_plane, 8, 2 * PAD), F32),
                pltpu.SemaphoreType.DMA((CHUNKS,)),
                pltpu.SemaphoreType.DMA((n_plane,)),
                pltpu.SemaphoreType.DMA((2,)),
                pltpu.SemaphoreType.DMA,
                pltpu.SemaphoreType.DMA((N_GROUPS,)),
                pltpu.SemaphoreType.DMA((N_GROUPS,)),
            ],
            compiler_params=pltpu.CompilerParams(
                collective_id=0, has_side_effects=True, vmem_limit_bytes=60 * 2**20
            ),
            name="sweep",
        )(right_sides, diag_tiles, left_factors, source_factors, trace_factors)
        return out.astype(F32)[None]

    placed = (
        P("slab", "plane", None),
        P("slab", None, "plane", None),
        P("slab", None, None, "plane"),
        P("slab", None, None, "plane"),
        P("slab", None, None, "plane"),
    )
    return jax.shard_map(
        body, mesh=mesh, in_specs=placed, out_specs=P("slab", "plane", None), check_vma=False
    )
```

```python
import functools

import jax
import jax.numpy as jnp
from jax import lax
from jax.experimental import pallas as pl
from jax.experimental.pallas import tpu as pltpu
from jax.sharding import PartitionSpec as P

MESH = pl.DeviceIdType.MESH
F32 = jnp.float32
BF16 = jnp.bfloat16
PAD = 128
CHUNKS = 8
X0, X1, T, RM, AM, RS, AV, E, U, MH, MS = 0, 1, 2, 3, 4, 5, 6, 7, 8, 15, 22
N_GROUPS = 29
PLAN = (1, 3)


def split(value):
    high = value.astype(BF16)
    low = (value - high.astype(F32)).astype(BF16)
    return high, low


def nt_dot(rows, mat):
    return lax.dot_general(rows, mat, (((1,), (1,)), ((), ())), preferred_element_type=F32)


def nn_dot(rows, mat):
    return lax.dot_general(rows, mat, (((1,), (0,)), ((), ())), preferred_element_type=F32)


def from_products(both):
    half = both.shape[0] // 2
    real = both[:half, :PAD] - both[half:, PAD:]
    imag = both[half:, :PAD] + both[:half, PAD:]
    return jnp.concatenate([real, imag], axis=1)


def moved(rows, *parts):
    count = rows.shape[0]
    upright = jnp.concatenate([rows[:, :PAD], rows[:, PAD:]], axis=0)
    stacked = stacked_halves(upright)
    both = sum(nn_dot(stacked, part) for part in parts)
    both = both[:2 * count] + both[2 * count:]
    return from_products(both)


def stacked_halves(rows):
    rows_high = rows.astype(BF16).astype(F32)
    return jnp.concatenate([rows_high, rows - rows_high], axis=0).astype(BF16)


def kernel(
    n_slab, n_plane, rank,
    rs_ref, d_ref, l_ref, sf_ref, t_ref, o_ref,
    d_vm, rs_vm, x_send, x_recv, t_own, t_vm, l_vm, sw_vm, local, e_send,
    m_part, m_recv, a1, earlier,
    c_part, c_recv, u_send, u_recv, mix,
    d_sem, rs_sem, in_sem, own_sem, send_sem, recv_sem,
):
    s = lax.axis_index("slab")
    p = lax.axis_index("plane")
    tile = d_ref.shape[2]
    step = tile // CHUNKS
    side = n_plane // 2
    run = max(1, n_plane // 8)

    my_side = lax.rem(lax.div(p, run), 2)
    my_slot = lax.div(p, 2 * run) * run + lax.rem(p, run)
    far_side = 1 - my_side
    me = my_side * side + my_slot

    def place(which, i):
        return which * side + lax.rem(my_slot + i, side)

    def device_at(k):
        slot = lax.rem(k, side)
        return lax.div(slot, run) * 2 * run + lax.div(k, side) * run + lax.rem(slot, run)

    by_distance = sorted(range(side), key=lambda i: -min(i, side - i))
    far = [(k, device_at(k)) for k in (place(far_side, i) for i in by_distance)]
    near = [(k, device_at(k)) for k in (place(my_side, i) for i in by_distance if i)]

    def remote(src, dst, group, device):
        return pltpu.make_async_remote_copy(
            src_ref=src, dst_ref=dst, send_sem=send_sem.at[group], recv_sem=recv_sem.at[group],
            device_id=device, device_id_type=MESH,
        )

    peer = (s, lax.rem(p + 1, n_plane))

    def await_recv(ref, group):
        remote(ref, ref, group, peer).wait_recv()

    def await_send(ref, group):
        remote(ref, ref, group, peer).wait_send()

    others = pl.ds(0, n_plane - 1)
    held = m_part.shape[1]
    n_owners = rank // held
    spread = [2 * i for i in range(3)] + [side + 2 * i for i in range(1, 4)]
    owner_places = spread if n_plane == 16 else list(range(n_owners))
    owner_devices = [(k % side) // run * 2 * run + k // side * run + k % side % run for k in owner_places]
    owner, my_rows = me < 0, jnp.int32(0)
    for j, k in enumerate(owner_places):
        owner = owner | (me == k)
        my_rows = my_rows + j * (me == k).astype(jnp.int32)
    all_rows = pl.ds(0, n_owners)
    near_others = pl.ds(0, side - 1)
    all_far = pl.ds(0, side)

    def to_plane(src, dst, group):
        for _, q in far + near:
            remote(src, dst, group, (s, q)).start()

    def blocks_to(targets, src, dst, group, slab):
        for k, q in targets:
            remote(src.at[k], dst, group, (slab, q)).start()

    own_t = pltpu.make_async_copy(t_ref.at[0], t_own, in_sem.at[2])
    own_t.start()

    barrier = pltpu.get_barrier_semaphore()

    def greet(device):
        pl.semaphore_signal(barrier, inc=1, device_id=device, device_id_type=MESH)

    def greet_plane(i, carry):
        greet((s, lax.rem(p + i, n_plane)))
        return carry
    lax.fori_loop(1, n_plane, greet_plane, 0)
    pl.when(s < n_slab - 1)(lambda: greet((s + 1, p)))
    for distance in range(1, n_slab):
        pl.when(s >= distance)(functools.partial(lambda d: greet((s - d, p)), distance))


    def rs_copy(k):
        lanes = pl.ds(pl.multiple_of(device_at(k) * tile, tile), tile)
        return pltpu.make_async_copy(rs_ref.at[0, :, lanes], rs_vm.at[k], rs_sem.at[k])

    def start_rs(which):
        def one(i, carry):
            rs_copy(place(which, i)).start()
            return carry
        lax.fori_loop(0, side, one, 0)

    start_rs(my_side)
    s_copy = pltpu.make_async_copy(sf_ref.at[0], sw_vm.at[pl.ds(0, 2), pl.ds(0, rank), :], in_sem.at[1])
    s_copy.start()

    def d_copy(j):
        rows = pl.ds(pl.multiple_of(j * step, step), step)
        return pltpu.make_async_copy(d_ref.at[0, :, rows, :], d_vm.at[:, rows, :], d_sem.at[j])

    def start_d(j, carry):
        d_copy(j).start()
        return carry

    start_rs(far_side)
    lax.fori_loop(0, CHUNKS, start_d, 0)
    l_copy = pltpu.make_async_copy(l_ref.at[0], l_vm.at[:, pl.ds(0, rank), :], in_sem.at[0])
    l_copy.start()
    for padded in (t_vm, l_vm, sw_vm):
        padded[pl.ds(0, 2), rank:, :] = jnp.zeros((2, PAD - rank, tile), BF16)


    @pl.when(s == n_slab - 1)
    def _():
        sw_vm[pl.ds(2, 4)] = jnp.zeros((4, PAD, tile), BF16)

    for slot in range(2):
        a1[slot, n_owners:] = jnp.zeros(a1.shape[1:], BF16)[n_owners:]
    for slot in range(n_slab - 1):
        for part in range(2):
            earlier[slot, part, n_owners:] = jnp.zeros(a1.shape[1:], BF16)[n_owners:]

    expected = n_plane - 1 + (s >= 1).astype(jnp.int32)
    for distance in range(1, n_slab):
        expected = expected + (s + distance < n_slab).astype(jnp.int32)
    pl.semaphore_wait(barrier, expected)

    own_t.wait()
    t_copy = remote(t_own, t_vm.at[:, pl.ds(0, rank), :], T, (s - 1, p))
    pl.when(s >= 1)(t_copy.start)

    for k, q in near:
        rs_copy(k).wait()
        x_send[k] = rs_vm[k].astype(BF16)
        remote(x_send.at[k], x_recv.at[me], X0, (s, q)).start()
    rs_copy(me).wait()
    x_recv[me] = rs_vm[me].astype(BF16)

    def far_cast(i, carry):
        k = place(far_side, i)
        rs_copy(k).wait()
        x_send[k] = rs_vm[k].astype(BF16)
        return carry
    lax.fori_loop(0, side, far_cast, 0)

    def side_rows(which):
        return pl.ds(which * side, side)

    def local_part(which, begin, end, first):
        def chunk(j, carry):
            if first:
                d_copy(j).wait()
            rows = pl.ds(pl.multiple_of(j * step, step), step)
            x = x_recv[side_rows(which)].reshape(side * 16, tile)
            real = nt_dot(d_vm[0, rows, :], x).T
            imag = nt_dot(d_vm[1, rows, :], x).T
            local[which, :side * 8, rows] = real[:side * 8] - imag[side * 8:]
            local[which, side * 8:, rows] = real[side * 8:] + imag[:side * 8]
            return carry
        lax.fori_loop(begin, end, chunk, 0)

    def trace_weights(first, last):
        def chunk(j, carry):
            rows = pl.ds(pl.multiple_of(j * step, step), step)
            t_rows = t_vm[...].reshape(2 * PAD, tile)
            with_real = nn_dot(t_rows, d_vm[0, :, rows])
            with_imag = nn_dot(t_rows, d_vm[1, :, rows])
            for part, value in enumerate((
                with_real[:PAD] - with_imag[PAD:], with_imag[:PAD] + with_real[PAD:]
            )):
                high, low = split(value)
                sw_vm[2 + part, :, rows] = high
                sw_vm[4 + part, :, rows] = low
            return carry
        lax.fori_loop(first, last, chunk, 0)

    def rank_part(which):
        x = x_recv[side_rows(which)].reshape(side * 16, tile)
        both = nt_dot(x, sw_vm[...].reshape(6 * PAD, tile))
        source = from_products(both[:, :2 * PAD])
        trace = from_products(both[:, 2 * PAD:4 * PAD] + both[:, 4 * PAD:])
        c_part[side_rows(which), 0] = source.reshape(side, 8, 2 * PAD)
        c_part[side_rows(which), 1] = trace.reshape(side, 8, 2 * PAD)

    await_recv(x_recv.at[near_others], X0)
    local_part(my_side, 0, CHUNKS, True)
    s_copy.wait()
    l_copy.wait()

    pl.when(s >= 1)(t_copy.wait_send)
    blocks_to(far, x_send, x_recv.at[me], X1, s)

    @pl.when(s < n_slab - 1)
    def _():
        t_copy.wait_recv()
        products = nt_dot(l_vm[...].reshape(2 * PAD, tile), t_vm[...].reshape(2 * PAD, tile))
        m_part[...] = from_products(products).reshape(m_part.shape)

        for j, q in enumerate(owner_devices):
            remote(m_part.at[j], m_recv.at[me], RM, (s + 1, q)).start()

    pl.when(s < n_slab - 1)(lambda: trace_weights(0, CHUNKS))

    def sum_m():
        @pl.when((s >= 1) & owner)
        def _():
            await_recv(m_recv, RM)
            high, low = split(jnp.sum(m_recv[...], axis=0))
            a1[0, my_rows] = high
            a1[1, my_rows] = low
            to_plane(a1.at[:, my_rows], a1.at[:, my_rows], AM)

    rank_part(my_side)
    c_recv[me] = c_part[me]
    blocks_to(near, c_part, c_recv.at[me], RS, s)
    sum_m()

    part = lax.rem(p, 2)
    partner = (s, p + 1 - 2 * part)
    later_copies = [
        (
            remote(a1.at[part, all_rows], earlier.at[d - 1, part, all_rows], MH + d - 1, (s + d, p)),
            (s >= 1) & (s + d < n_slab),
        )
        for d in range(1, n_slab)
    ]
    shared_copies = [
        remote(earlier.at[d - 1, part, all_rows], earlier.at[d - 1, part, all_rows], MS + d - 1, partner)
        for d in range(1, n_slab)
    ]

    def send_later():
        @pl.when(s >= 1)
        def _():
            pl.when(owner)(lambda: await_recv(a1.at[:, pl.ds(0, n_owners - 1)], AM))
            pl.when(jnp.logical_not(owner))(lambda: await_recv(a1.at[:, all_rows], AM))
            for copy, needed in later_copies:
                pl.when(needed)(copy.start)

    await_recv(x_recv.at[all_far], X1)
    rank_part(far_side)
    blocks_to(far, c_part, c_recv.at[me], RS, s)

    send_later()

    before_sums, before_scan = PLAN[0], PLAN[0] + PLAN[1]
    local_part(far_side, 0, before_sums, False)
    await_recv(c_recv.at[others], RS)
    u_send[...] = jnp.sum(c_recv[...], axis=0)
    u_copies = []
    for distance in range(1, n_slab):
        copy = remote(u_send, u_recv.at[distance - 1], U + distance - 1, (s + distance, p))
        u_copies.append(copy)
        pl.when(s + distance < n_slab)(copy.start)
    local_part(far_side, before_sums, before_scan, False)
    for d in range(1, n_slab - 1):
        @pl.when(s > d)
        def _():
            later_copies[d - 1][0].wait_recv()
            shared_copies[d - 1].start()

    def await_u(distance):
        remote(u_send, u_recv.at[0], U + distance - 1, peer).wait_recv()

    mix[me] = u_send[0]

    @pl.when(s >= 1)
    def _():
        await_u(s)

        def advance(step_back, value):
            d = s - step_back
            await_u(d)
            remote(a1.at[0, all_rows], earlier.at[0, 0, all_rows], MS + d - 1, peer).wait_recv()
            high, low = earlier[d - 1, 0].reshape(PAD, 2 * PAD), earlier[d - 1, 1].reshape(PAD, 2 * PAD)
            return u_recv[d - 1, 0] + u_recv[d, 1] + moved(value, high, low)
        value = lax.fori_loop(1, s, advance, u_recv[s - 1, 0])
        high, low = a1[0].reshape(PAD, 2 * PAD), a1[1].reshape(PAD, 2 * PAD)
        mix[me] = u_send[0] + u_recv[0, 1] + moved(value, high, low)

    to_plane(mix.at[me], mix.at[me], AV)
    local_part(far_side, before_scan, CHUNKS, False)
    await_recv(mix.at[others], AV)

    mine = pl.ds(pl.multiple_of(p * tile, tile), tile)

    def solve_side(which):
        mixing = mix[side_rows(which)].reshape(side * 8, 2 * PAD)
        real, imag = mixing[:, :PAD], mixing[:, PAD:]
        square = jnp.concatenate(
            [jnp.concatenate([real, -imag], axis=1), jnp.concatenate([imag, real], axis=1)], axis=0
        )
        both = nn_dot(stacked_halves(square), l_vm[...].reshape(2 * PAD, tile))
        solved = local[which] + both[:side * 16] + both[side * 16:]
        e_send[side_rows(which)] = solved.astype(BF16).reshape(side, 16, tile)

    solve_side(far_side)
    blocks_to(far, e_send, o_ref.at[:, mine], E, s)
    solve_side(my_side)
    blocks_to(near, e_send, o_ref.at[:, mine], E, s)
    own = pltpu.make_async_copy(e_send.at[me], o_ref.at[:, mine], own_sem)
    own.start()

    await_send(x_send.at[near_others], X0)
    await_send(x_send.at[all_far], X1)
    await_send(c_part.at[others], RS)
    await_send(mix.at[others], AV)

    @pl.when(s < n_slab - 1)
    def _():
        await_send(m_part.at[all_rows], RM)

    pl.when((s >= 1) & owner)(lambda: await_send(m_recv.at[others], AM))
    for copy, needed in later_copies:
        pl.when(needed)(copy.wait_send)
    for d in range(1, n_slab - 1):
        pl.when(s > d)(shared_copies[d - 1].wait_send)
    for distance in range(1, n_slab):
        pl.when(s + distance < n_slab)(u_copies[distance - 1].wait_send)
    own.wait()
    await_send(e_send.at[others], E)
    await_recv(o_ref.at[:, pl.ds(0, (n_plane - 1) * tile)], E)


def solution(mesh):
    n_slab, n_plane = mesh.shape["slab"], mesh.shape["plane"]

    def body(right_sides, diag_tiles, left_factors, source_factors, trace_factors):
        tile, rank = diag_tiles.shape[2], left_factors.shape[2]
        columns = right_sides.shape[1]
        held = 16 if n_plane == 16 else 32
        pairs = pltpu.VMEM((n_plane, 2, 8, 2 * PAD), F32)
        padded = pltpu.VMEM((2, PAD, tile), BF16)
        blocks = pltpu.VMEM((n_plane, columns, tile), BF16)
        out = pl.pallas_call(
            functools.partial(kernel, n_slab, n_plane, rank),
            out_shape=jax.ShapeDtypeStruct((columns, n_plane * tile), BF16),
            in_specs=[pl.BlockSpec(memory_space=pl.ANY)] * 5,
            out_specs=pl.BlockSpec(memory_space=pl.ANY),
            scratch_shapes=[
                pltpu.VMEM((2, tile, tile), BF16),
                pltpu.VMEM((n_plane, columns, tile), F32),
                blocks, blocks, pltpu.VMEM((2, rank, tile), BF16), padded, padded, pltpu.VMEM((6, PAD, tile), BF16),
                pltpu.VMEM((2, columns * n_plane // 2, tile), F32),
                blocks,
                pltpu.VMEM((PAD // held, held, 2 * PAD), F32),
                pltpu.VMEM((n_plane, held, 2 * PAD), F32),
                pltpu.VMEM((2, PAD // held, held, 2 * PAD), BF16),
                pltpu.VMEM((n_slab - 1, 2, PAD // held, held, 2 * PAD), BF16),
                pairs, pairs,
                pltpu.VMEM((2, 8, 2 * PAD), F32),
                pltpu.VMEM((n_slab - 1, 2, 8, 2 * PAD), F32),
                pltpu.VMEM((n_plane, 8, 2 * PAD), F32),
                pltpu.SemaphoreType.DMA((CHUNKS,)),
                pltpu.SemaphoreType.DMA((n_plane,)),
                pltpu.SemaphoreType.DMA((3,)),
                pltpu.SemaphoreType.DMA,
                pltpu.SemaphoreType.DMA((N_GROUPS,)),
                pltpu.SemaphoreType.DMA((N_GROUPS,)),
            ],
            compiler_params=pltpu.CompilerParams(
                collective_id=0, has_side_effects=True, vmem_limit_bytes=60 * 2**20
            ),
            name="sweep",
        )(right_sides, diag_tiles, left_factors, source_factors, trace_factors)
        return out.astype(F32)[None]

    placed = (
        P("slab", "plane", None),
        P("slab", None, "plane", None),
        P("slab", None, None, "plane"),
        P("slab", None, None, "plane"),
        P("slab", None, None, "plane"),
    )
    return jax.shard_map(
        body, mesh=mesh, in_specs=placed, out_specs=P("slab", "plane", None), check_vma=False
    )
```
